32 devices in a mesh: rep: 4 (over y, x), wide: 8 (over z, core).
Axes of the slice: x: 2, y: 2, z: 4, core: 2. Of those that a mesh axis runs over, the one named last changes fastest.
Arguments:
- decoder_input: bfloat16 [32, 1024, 512], P(('rep', 'wide')), may hold values from -6 to 6
- target_embed: bfloat16 [32, 1024, 512], P(('rep', 'wide')), may hold values from -6 to 6
- encoder_states: bfloat16 [32, 1024, 512], P(('rep', 'wide')), may hold values from -6 to 6
- sentence_ids: int32 [32, 1024], P(('rep', 'wide')), may hold values from 0 to 15, never falling along the last dimension, each value on 1 to 128 neighbouring positions
- position_ranks: int32 [32, 1024], P(('rep', 'wide')), may hold values from 0 to 127
- hamming_counts: int32 [32, 16], P(('rep', 'wide')), may hold values from 0 to 256
- output_grad: bfloat16 [32, 1024, 512], P(('rep', 'wide')), may hold values from -6 to 6
- attn_in: float32 [6, 512, 512], P(None, 'wide'), may hold values from -0.25 to 0.25
- attn_out: float32 [2, 512, 512], P(None, 'wide'), may hold values from -0.75 to 0.75
- ffn_in: float32 [1, 512, 2048], P(None, 'wide'), may hold values from -0.25 to 0.25
- ffn_out: float32 [1, 2048, 512], P(None, 'wide'), may hold values from -0.125 to 0.125
- small_params: float32 [11, 512], P(None, 'wide'), may hold values from -1.2 to 1.3, as said below
- attn_in_mom: float32 [6, 512, 512], P(None, 'wide'), may hold values from -0.3 to 0.3
- attn_out_mom: float32 [2, 512, 512], P(None, 'wide'), may hold values from -0.3 to 0.3
- ffn_in_mom: float32 [1, 512, 2048], P(None, 'wide'), may hold values from -0.3 to 0.3
- ffn_out_mom: float32 [1, 2048, 512], P(None, 'wide'), may hold values from -0.3 to 0.3
- small_mom: float32 [11, 512], P(None, 'wide'), may hold values from -0.3 to 0.3
- attn_in_err: float32 [4, 6, 512, 512], P('rep', None, 'wide'), may hold values from -5 to 5
- attn_out_err: float32 [4, 2, 512, 512], P('rep', None, 'wide'), may hold values from -5 to 5
- ffn_in_err: float32 [4, 1, 512, 2048], P('rep', None, 'wide'), may hold values from -5 to 5
- ffn_out_err: float32 [4, 1, 2048, 512], P('rep', None, 'wide'), may hold values from -5 to 5
- attn_in_fac: float32 [6, 512, 8], replicated, may hold values from -6 to 6
- attn_out_fac: float32 [2, 512, 8], replicated, may hold values from -6 to 6
- ffn_in_fac: float32 [1, 2048, 8], replicated, may hold values from -6 to 6
- ffn_out_fac: float32 [1, 512, 8], replicated, may hold values from -6 to 6
- attn_in_avg: float32 [6, 512, 512], P(None, 'wide'), may hold values from -0.25 to 0.25
- attn_out_avg: float32 [2, 512, 512], P(None, 'wide'), may hold values from -0.75 to 0.75
- ffn_in_avg: float32 [1, 512, 2048], P(None, 'wide'), may hold values from -0.25 to 0.25
- ffn_out_avg: float32 [1, 2048, 512], P(None, 'wide'), may hold values from -0.125 to 0.125
- small_avg: float32 [11, 512], P(None, 'wide'), may hold values from -1.2 to 1.3, as said below
Outputs:
- layer_out: bfloat16 [32, 1024, 512], P(('rep', 'wide'))
- input_grad: float32 [32, 1024, 512], P(('rep', 'wide'))
- attn_in_new: float32 [6, 512, 512], P(None, 'wide')
- attn_out_new: float32 [2, 512, 512], P(None, 'wide')
- ffn_in_new: float32 [1, 512, 2048], P(None, 'wide')
- ffn_out_new: float32 [1, 2048, 512], P(None, 'wide')
- small_new: float32 [11, 512], P(None, 'wide')
- attn_in_mom_new: float32 [6, 512, 512], P(None, 'wide')
- attn_out_mom_new: float32 [2, 512, 512], P(None, 'wide')
- ffn_in_mom_new: float32 [1, 512, 2048], P(None, 'wide')
- ffn_out_mom_new: float32 [1, 2048, 512], P(None, 'wide')
- small_mom_new: float32 [11, 512], P(None, 'wide')
- attn_in_err_new: float32 [4, 6, 512, 512], P('rep', None, 'wide')
- attn_out_err_new: float32 [4, 2, 512, 512], P('rep', None, 'wide')
- ffn_in_err_new: float32 [4, 1, 512, 2048], P('rep', None, 'wide')
- ffn_out_err_new: float32 [4, 1, 2048, 512], P('rep', None, 'wide')
- attn_in_fac_new: float32 [6, 512, 8], replicated
- attn_out_fac_new: float32 [2, 512, 8], replicated
- ffn_in_fac_new: float32 [1, 2048, 8], replicated
- ffn_out_fac_new: float32 [1, 512, 8], replicated
- attn_in_avg_new: float32 [6, 512, 512], P(None, 'wide')
- attn_out_avg_new: float32 [2, 512, 512], P(None, 'wide')
- ffn_in_avg_new: float32 [1, 512, 2048], P(None, 'wide')
- ffn_out_avg_new: float32 [1, 2048, 512], P(None, 'wide')
- small_avg_new: float32 [11, 512], P(None, 'wide')
The draws below stay inside these ranges and needn't reach their ends.
Inputs may be any that keep to these rules, and one draw needn't show every extreme that they name: `small_params`: rows 0, 2 and 4 are the gains, within 0.7 to 1.3; the other rows are shifts and biases. `small_avg`: rows 0, 2 and 4 are the gains' averages, within 0.7 to 1.3.
All inputs are finite; a program needn't handle non-finite values.
Results may differ from the reference program's by a relative error of at most 0.02.
The reference program's roundings to bfloat16 on the way count: a program that leaves them out, or rounds other values in their place, can miss the bound.
Values may be sent and summed in bfloat16 or wider, within the bound.
A program may use at most 320 MiB of HBM per device.

```python
import math
import jax
import jax.numpy as jnp
import numpy as np
from jax import lax

D = 512
HEADS = 8
HEAD_DIM = 64
FF = 2048
TOK = 1024
SENTS = 16
MOST = 128
RANK = 8
ROWS = 32
GROUP_TOK = 8192
SMALL_ROWS = 11
N_REP = 4
N_WIDE = 8


def small_table(key):
    row_index = lax.broadcasted_iota(jnp.int32, (SMALL_ROWS, D), 0)
    spread = jax.random.uniform(jax.random.fold_in(key, 1), (SMALL_ROWS, D), jnp.float32, -1.0, 1.0)
    normal_part = jnp.clip(jax.random.normal(jax.random.fold_in(key, 2), (SMALL_ROWS, D), jnp.float32), -4.0, 4.0)
    gain_rows = (row_index == 0) | (row_index == 2) | (row_index == 4)
    return jnp.where(gain_rows, 1.0 + 0.3 * spread, 0.3 * normal_part)


def draw_small_params(key, part):
    return small_table(jax.random.fold_in(key, 11))


def draw_small_avg(key, part):
    return small_table(jax.random.fold_in(key, 23))


def touch_ends(entries, key, low, largest):
    shape = entries.shape
    index_at = [jax.random.randint(jax.random.fold_in(key, axis), (), 0, shape[axis]) for axis in range(len(shape))]
    entries = entries.at[tuple(index_at)].set(low)
    longest = shape.index(max(shape))
    index_at[longest] = (index_at[longest] + 1) % shape[longest]
    return entries.at[tuple(index_at)].set(largest)


def levels(rng, dims, shards, least, high):
    loudness, own = 1.0, jax.random.fold_in(rng, 6)
    for dim, blocks in shards:
        steps = jnp.exp(jax.random.uniform(jax.random.fold_in(own, dim), (blocks,), jnp.float32, least / len(shards), high / len(shards)))
        loudness = loudness * jnp.repeat(steps, dims[dim] // blocks).reshape([-1 if axis == dim else 1 for axis in range(len(dims))])
    return loudness


def profile(number_of, total, reach, slope):
    loads = [(1 << 20) // math.isqrt(grade ** slope) + 1 for grade in range(2, number_of + 1)]
    surplus, counts = total - reach - (number_of - 1), [1] * (number_of - 1)
    while surplus > 0:
        movable = [i for i in range(number_of - 1) if counts[i] < reach]
        whole, remaining = sum([loads[i] for i in movable]), surplus
        for i in movable:
            extra = min(reach - counts[i], max(1, remaining * loads[i] // whole), surplus)
            counts[i] = counts[i] + extra
            surplus = surplus - extra
    return np.array([reach] + counts)


def uneven_parts(stream_key, count, total, limit, lean):
    if count == 2:
        one = jax.random.randint(stream_key, (), max(1, total - limit), min(limit, total - 1) + 1)
        return jnp.stack([one, total - one])
    lengths = jnp.asarray(profile(count, total, limit, lean), jnp.int32)
    pairs = (count - 1) // 2
    source_of, sink = lengths[1:1 + 2 * pairs:2], lengths[2:2 + 2 * pairs:2]
    margin = jnp.minimum(source_of - 1, limit - sink)
    shifted = jax.random.randint(jax.random.fold_in(stream_key, 1), (pairs,), 0, 1 << 20) % (margin + 1)
    lengths = lengths.at[1:1 + 2 * pairs:2].set(source_of - shifted).at[2:2 + 2 * pairs:2].set(sink + shifted)
    return lengths[jax.random.permutation(jax.random.fold_in(stream_key, 2), count)]


def bell_draw(own_key, shape, deviation, bound, pieces=(), dtype=jnp.bfloat16):
    result = jax.random.normal(own_key, shape, jnp.float32) * deviation
    if len(pieces) > 0:
        result = levels(own_key, shape, pieces, -0.22, 0.18) * result
    return jnp.clip(result, min=-bound, max=bound).astype(dtype)


def setup_inputs(seed: int = 0) -> dict:
    key_of = jax.random.split(jax.random.key(seed), 31)
    return {
        "decoder_input": bell_draw(key_of[0], (ROWS, TOK, D), 1.0, 6.0, ((0, 32),)),
        "target_embed": bell_draw(key_of[1], (ROWS, TOK, D), 1.0, 6.0, ((0, 32),)),
        "encoder_states": bell_draw(key_of[2], (ROWS, TOK, D), 1.0, 6.0, ((0, 32),)),
        "sentence_ids": jax.vmap(lambda own: jnp.searchsorted(jnp.cumsum(uneven_parts(own, SENTS, TOK, MOST, 0)), jnp.arange(TOK), side="right"))(jax.random.split(key_of[3], ROWS)).reshape((ROWS, TOK)).astype(jnp.int32),
        "position_ranks": touch_ends(jax.random.randint(key_of[4], (ROWS, TOK), 0, MOST), jax.random.fold_in(key_of[4], 1), 0, MOST - 1).astype(jnp.int32),
        "hamming_counts": touch_ends(jax.random.randint(key_of[5], (ROWS, SENTS), 0, 2 * MOST + 1), jax.random.fold_in(key_of[5], 1), 0, 2 * MOST).astype(jnp.int32),
        "output_grad": bell_draw(key_of[6], (ROWS, TOK, D), 1.0, 6.0, ((0, 32),)),
        "attn_in": bell_draw(key_of[7], (6, D, D), D ** -0.5, 0.25, ((1, 8),), jnp.float32),
        "attn_out": bell_draw(key_of[8], (2, D, D), (D // 8) ** -0.5, 0.75, ((1, 8),), jnp.float32),
        "ffn_in": bell_draw(key_of[9], (1, D, FF), D ** -0.5, 0.25, ((1, 8),), jnp.float32),
        "ffn_out": bell_draw(key_of[10], (1, FF, D), FF ** -0.5, 0.125, ((1, 8),), jnp.float32),
        "small_params": draw_small_params(jax.random.fold_in(key_of[30], 71), 0),
        "attn_in_mom": bell_draw(key_of[12], (6, D, D), 0.05, 0.3, ((1, 8),), jnp.float32),
        "attn_out_mom": bell_draw(key_of[13], (2, D, D), 0.05, 0.3, ((1, 8),), jnp.float32),
        "ffn_in_mom": bell_draw(key_of[14], (1, D, FF), 0.05, 0.3, ((1, 8),), jnp.float32),
        "ffn_out_mom": bell_draw(key_of[15], (1, FF, D), 0.05, 0.3, ((1, 8),), jnp.float32),
        "small_mom": bell_draw(key_of[16], (SMALL_ROWS, D), 0.05, 0.3, ((1, 8),), jnp.float32),
        "attn_in_err": bell_draw(key_of[17], (N_REP, 6, D, D), 1.0, 5.0, ((0, 4), (2, 8)), jnp.float32),
        "attn_out_err": bell_draw(key_of[18], (N_REP, 2, D, D), 1.0, 5.0, ((0, 4), (2, 8)), jnp.float32),
        "ffn_in_err": bell_draw(key_of[19], (N_REP, 1, D, FF), 1.0, 5.0, ((0, 4), (2, 8)), jnp.float32),
        "ffn_out_err": bell_draw(key_of[20], (N_REP, 1, FF, D), 1.0, 5.0, ((0, 4), (2, 8)), jnp.float32),
        "attn_in_fac": bell_draw(key_of[21], (6, D, RANK), 1.0, 6.0, (), jnp.float32),
        "attn_out_fac": bell_draw(key_of[22], (2, D, RANK), 1.0, 6.0, (), jnp.float32),
        "ffn_in_fac": bell_draw(key_of[23], (1, FF, RANK), 1.0, 6.0, (), jnp.float32),
        "ffn_out_fac": bell_draw(key_of[24], (1, D, RANK), 1.0, 6.0, (), jnp.float32),
        "attn_in_avg": bell_draw(key_of[25], (6, D, D), D ** -0.5, 0.25, ((1, 8),), jnp.float32),
        "attn_out_avg": bell_draw(key_of[26], (2, D, D), (D // 8) ** -0.5, 0.75, ((1, 8),), jnp.float32),
        "ffn_in_avg": bell_draw(key_of[27], (1, D, FF), D ** -0.5, 0.25, ((1, 8),), jnp.float32),
        "ffn_out_avg": bell_draw(key_of[28], (1, FF, D), FF ** -0.5, 0.125, ((1, 8),), jnp.float32),
        "small_avg": draw_small_avg(jax.random.fold_in(key_of[30], 71), 0),
    }


FULL_PRECISION = lax.Precision.HIGHEST
MOMENTUM = 0.9
LEARN_RATE = 0.1
VECTOR_RATE = 0.5
AVERAGE = 0.25

@jax.custom_vjp
def low(v):
    return lax.optimization_barrier(v.astype(jnp.bfloat16)).astype(jnp.float32)

@jax.custom_vjp
def low_back(v):
    return v

def low_keep(v):
    return (low(v), None)

def low_pass(kept, grad):
    return (grad,)

def back_keep(v):
    return (v, None)

def back_low(kept, grad):
    return (low(grad),)
low.defvjp(low_keep, low_pass)
low_back.defvjp(back_keep, back_low)

def matmul(left_arr, right_arr):
    return jnp.dot(left_arr.astype(jnp.float32), right_arr.astype(jnp.float32), precision=FULL_PRECISION, preferred_element_type=jnp.float32)

def gelu_exact(value):
    return 0.5 * value * (1.0 + lax.erf(value * 0.7071067811865476))

def layer_norm(resid, gain, shift):
    center = resid - lax.optimization_barrier(jnp.mean(resid, axis=-1, keepdims=True))
    variance = lax.optimization_barrier(jnp.mean(center * center, axis=-1, keepdims=True))
    return center * lax.rsqrt(variance + 1e-05) * gain + shift

def attention(query_in, source, w_query, w_key, w_value, w_out, same_sentence):
    length = query_in.shape[0]
    block_rows = min(512, length)
    score_scale = HEAD_DIM ** (-0.5)
    query_proj = low_back(low(matmul(query_in, w_query))).reshape(length // block_rows, block_rows, HEADS, HEAD_DIM)
    key_proj = low_back(low(matmul(source, w_key))).reshape(length, HEADS, HEAD_DIM)
    value_proj = low_back(low(matmul(source, w_value))).reshape(length, HEADS, HEAD_DIM)
    mask_rows = same_sentence.reshape(length // block_rows, block_rows, length)

    def score_block(inputs):
        query_block, mask_block = inputs
        scores = jnp.einsum('qhd,khd->hqk', query_block, key_proj, precision=FULL_PRECISION) * score_scale
        scores = low_back(jnp.where(mask_block[None], scores, -1000000000.0))
        attn_probs = low(jax.nn.softmax(scores, axis=-1))
        return jnp.einsum('hqk,khd->qhd', attn_probs, value_proj, precision=FULL_PRECISION)
    mixed_out = lax.map(jax.checkpoint(score_block), (query_proj, mask_rows)).reshape(length, HEADS * HEAD_DIM)
    mixed_out = low_back(low(mixed_out))
    return low_back(matmul(mixed_out, w_out))

def layer(params, mixed_in, encoder, same_sentence):
    attn_w, out_w, first_w, second_w, small_w = [low(weight) for weight in params]
    input_low = low(mixed_in)
    encoder_low = low(encoder)
    self_branch = attention(input_low, input_low, attn_w[0], attn_w[1], attn_w[2], out_w[0], same_sentence)
    hidden_one = layer_norm(mixed_in + self_branch, small_w[0], small_w[1])
    hidden_one_low = low(hidden_one)
    cross_branch = attention(hidden_one_low, encoder_low, attn_w[3], attn_w[4], attn_w[5], out_w[1], same_sentence)
    hidden_two = layer_norm(hidden_one + cross_branch, small_w[2], small_w[3])
    hidden_two_low = low(hidden_two)
    inner_pre = low_back(matmul(hidden_two_low, first_w[0]) + small_w[7:].reshape(FF))
    act_out = low(gelu_exact(inner_pre))
    ffn_branch = low_back(matmul(act_out, second_w[0]) + small_w[6])
    return layer_norm(hidden_two + ffn_branch, small_w[4], small_w[5])

def row_grads(params, decoder_row, target_row, encoder_row, sentence, position, hamming, cotangent):
    same_sentence = sentence[:, None] == sentence[None, :]
    labels = lax.broadcasted_iota(jnp.int32, (1, SENTS), 1)
    per_pos = lax.optimization_barrier(jnp.sum(jnp.where(sentence[:, None] == labels, hamming[None, :], 0), axis=1))
    glance = 2 * position < per_pos
    mixed_in = jnp.where(glance[:, None], target_row, decoder_row).astype(jnp.float32)
    encoder = encoder_row.astype(jnp.float32)
    row_out, pullback = jax.vjp(lambda weights, inputs: layer(weights, inputs, encoder, same_sentence), params, mixed_in)
    gradients, in_grad = pullback(cotangent.astype(jnp.float32))
    return (row_out, gradients, in_grad)

def reference(decoder_input, target_embed, encoder_states, sentence_ids, position_ranks, hamming_counts, output_grad, attn_in, attn_out, ffn_in, ffn_out, small_params, attn_in_mom, attn_out_mom, ffn_in_mom, ffn_out_mom, small_mom, attn_in_err, attn_out_err, ffn_in_err, ffn_out_err, attn_in_fac, attn_out_fac, ffn_in_fac, ffn_out_fac, attn_in_avg, attn_out_avg, ffn_in_avg, ffn_out_avg, small_avg):
    params = (attn_in, attn_out, ffn_in, ffn_out, small_params)
    row_arrays = tuple((item.reshape((N_REP, N_WIDE) + item.shape[1:]) for item in (decoder_input, target_embed, encoder_states, sentence_ids, position_ranks, hamming_counts, output_grad)))

    def replica(rows_of_group):

        def one_row(running, row_data):
            row_out, gradients, in_grad = row_grads(params, *row_data)
            running = jax.tree.map(lambda acc, new: acc + new, running, gradients)
            return (running, (row_out.astype(jnp.bfloat16), in_grad))
        zero_sums = jax.tree.map(lambda weight: jnp.zeros(weight.shape, jnp.float32), params)
        return lax.scan(one_row, zero_sums, rows_of_group)
    group_sums, (outputs, in_grads) = lax.map(replica, row_arrays)
    scaling = GROUP_TOK ** (-0.5)
    group_sums = [piece * scaling for piece in group_sums]
    matrices = [(group_sums[0], attn_in_err, attn_in_fac), (group_sums[1], attn_out_err, attn_out_fac), (group_sums[2], ffn_in_err, ffn_in_fac), (group_sums[3], ffn_out_err, ffn_out_fac)]
    reduced, new_errors, new_factors = ([], [], [])
    for gradient, error, factor_in in matrices:
        full_grad = gradient + error
        left_mean = lax.optimization_barrier(jnp.sum(jnp.einsum('rknm,kmq->rknq', full_grad, factor_in, precision=FULL_PRECISION), axis=0)) / N_REP
        gram = jnp.einsum('knq,kns->kqs', left_mean, left_mean, precision=FULL_PRECISION)
        cholesky_factor = jnp.linalg.cholesky(gram)
        orthonormal = jnp.swapaxes(jax.scipy.linalg.solve_triangular(cholesky_factor, jnp.swapaxes(left_mean, 1, 2), lower=True), 1, 2)
        right_mean = lax.optimization_barrier(jnp.sum(jnp.einsum('rknm,knq->rkmq', full_grad, orthonormal, precision=FULL_PRECISION), axis=0)) / N_REP
        approx = jnp.einsum('knq,kmq->knm', orthonormal, right_mean, precision=FULL_PRECISION)
        reduced.append(approx)
        new_errors.append(full_grad - approx[None])
        new_factors.append(right_mean)
    reduced.append(lax.optimization_barrier(jnp.sum(group_sums[4], axis=0)) / N_REP)
    momenta = (attn_in_mom, attn_out_mom, ffn_in_mom, ffn_out_mom, small_mom)
    averages = (attn_in_avg, attn_out_avg, ffn_in_avg, ffn_out_avg, small_avg)
    rates = (LEARN_RATE, LEARN_RATE, LEARN_RATE, LEARN_RATE, VECTOR_RATE)
    new_weights, new_momenta, new_averages = ([], [], [])
    for master, moment, average, update, rate in zip(params, momenta, averages, reduced, rates):
        moment_new = MOMENTUM * moment + update
        weight_new = master - rate * moment_new
        new_weights.append(weight_new)
        new_momenta.append(moment_new)
        new_averages.append(average + AVERAGE * (weight_new - average))
    return (outputs.reshape(ROWS, TOK, D), in_grads.reshape(ROWS, TOK, D), new_weights[0], new_weights[1], new_weights[2], new_weights[3], new_weights[4], new_momenta[0], new_momenta[1], new_momenta[2], new_momenta[3], new_momenta[4], new_errors[0], new_errors[1], new_errors[2], new_errors[3], new_factors[0], new_factors[1], new_factors[2], new_factors[3], new_averages[0], new_averages[1], new_averages[2], new_averages[3], new_averages[4])
```

```python
import jax
import jax.numpy as jnp
from jax import lax
from jax.experimental import pallas as pl
from jax.experimental.pallas import tpu as pltpu
from jax.sharding import PartitionSpec as P

HEADS = 8
HEAD_DIM = 64
BLOCK = 256
SPAN = 128
EPS = 1e-05
BF = jnp.bfloat16
F32 = jnp.float32


FULL_PRECISION = lax.Precision.HIGHEST
MOMENTUM = 0.9
LEARN_RATE = 0.1
VECTOR_RATE = 0.5
AVERAGE = 0.25


def dot(a, b):
    return lax.dot_general(a, b, (((1,), (0,)), ((), ())), preferred_element_type=F32)


def dot_nt(a, b):
    return lax.dot_general(a, b, (((1,), (1,)), ((), ())), preferred_element_type=F32)


def dot_tn(a, b):
    return lax.dot_general(a, b, (((0,), (0,)), ((), ())), preferred_element_type=F32)


def gelu_pair(u):
    half = 0.5 * (1.0 + lax.erf(u * 0.7071067811865476))
    return u * half, half + u * jnp.exp(-0.5 * u * u) * 0.3989422804014327


def wide4(col):
    return jnp.concatenate([col] * 4, axis=1)


def norm_parts(resid):
    center = resid - jnp.mean(resid, axis=-1, keepdims=True)
    inv = lax.rsqrt(jnp.mean(center * center, axis=-1, keepdims=True) + EPS)
    return center * inv, inv


def norm_back(up, gain, normed, inv):
    scaled = up * gain
    return inv * (
        scaled
        - jnp.mean(scaled, axis=-1, keepdims=True)
        - normed * jnp.mean(scaled * normed, axis=-1, keepdims=True)
    )


def window(i, length):
    start = max(0, i * BLOCK - SPAN)
    return start, min(length, (i + 1) * BLOCK + SPAN) - start


def head_masks(rows):
    lane = lax.broadcasted_iota(jnp.int32, (rows, 2 * HEAD_DIM), 1)
    return lane < HEAD_DIM


def split_heads(pair, first):
    zero = jnp.zeros_like(pair)
    return jnp.where(first, pair, zero), jnp.where(first, zero, pair)


def attend(q, k, v_t, o, lse, bias, length):
    for i in range(length // BLOCK):
        start, wide = window(i, length)
        rows, keys = pl.ds(i * BLOCK, BLOCK), pl.ds(start, wide)

        @pl.loop(0, HEADS // 2)
        def _(pair):
            lanes = pl.ds(pl.multiple_of(pair * 128, 128), 128)
            k_pair = k[keys, lanes]
            first = head_masks(BLOCK)
            outs = []
            for which, q_head in enumerate(split_heads(q[rows, lanes], first)):
                s = dot_nt(k_pair, q_head) + bias[i, pl.ds(0, wide), :]
                peak = jnp.max(s, axis=0, keepdims=True)
                e = jnp.exp(s - peak)
                total = jnp.sum(e, axis=0, keepdims=True)
                p = (e * (1.0 / total)).astype(BF)
                head = pl.ds(pl.multiple_of(pair * 128 + which * 64, 64), 64)
                outs.append(dot(v_t[head, keys], p))
                lse[pl.ds(pair * 2 + which, 1), rows] = peak + jnp.log(total)
            o[rows, lanes] = jnp.concatenate(outs, axis=0).T.astype(BF)


def attend_back(q, k, v, k_t, do, lse, bias, dq, dk, dv, length):
    dk[...] = jnp.zeros_like(dk)
    dv[...] = jnp.zeros_like(dv)
    for i in range(length // BLOCK):
        start, wide = window(i, length)
        rows, keys = pl.ds(i * BLOCK, BLOCK), pl.ds(start, wide)

        @pl.loop(0, HEADS // 2)
        def _(pair):
            lanes = pl.ds(pl.multiple_of(pair * 128, 128), 128)
            k_pair, v_pair = k[keys, lanes], v[keys, lanes]
            first = head_masks(BLOCK)
            q_heads = split_heads(q[rows, lanes], first)
            d_heads = split_heads(do[rows, lanes], first)
            dq_t, dk_sum, dv_sum = [], None, None
            for which in range(2):
                s = dot_nt(k_pair, q_heads[which]) + bias[i, pl.ds(0, wide), :]
                p = jnp.exp(s - lse[pl.ds(pair * 2 + which, 1), rows])
                dp = dot_nt(v_pair, d_heads[which])
                diag = jnp.sum(p * dp, axis=0, keepdims=True)
                ds = (p * (dp - diag)).astype(BF)
                head = pl.ds(pl.multiple_of(pair * 128 + which * 64, 64), 64)
                dq_t.append(dot(k_t[head, keys], ds))
                dk_one = dot(ds, q_heads[which])
                dv_one = dot(p.astype(BF), d_heads[which])
                dk_sum = dk_one if dk_sum is None else dk_sum + dk_one
                dv_sum = dv_one if dv_sum is None else dv_sum + dv_one
            dq[rows, lanes] = (jnp.concatenate(dq_t, axis=0).T * HEAD_DIM ** (-0.5)).astype(BF)
            dk[keys, lanes] += dk_sum
            dv[keys, lanes] += dv_sum


def layer_kernel(
    sid, rank, ham, dec, tgt, enc, og,
    wa1, wo1, wa2, wo2, w1, w2, small,
    layer_out, in_grad, g1, g2, go2, ga2, go1, ga1, small_grad,
    x, q1, k1, v1, o1, q2, k2, v2, o2, turn, n1, n2, inv1, inv2,
    hid, du, dz, h2b, slope, da, do, bias, lse1, lse2, col,
):
    length, width = x.shape
    blocks = length // BLOCK
    scale = HEAD_DIM ** (-0.5)
    row = lambda r: small[pl.ds(r, 1), :]

    sent = sid[...]
    per_pos = jnp.zeros_like(sent)
    for s in range(ham.shape[1]):
        per_pos = jnp.where(sent == s, ham[0, s], per_pos)
    glance = jnp.where(2 * rank[...] < per_pos, 1.0, 0.0).astype(F32)
    sent_f = sent.astype(F32)
    col[...] = jnp.broadcast_to(glance, (128, length)).T

    @pl.loop(0, blocks)
    def _(i):
        rows = pl.ds(pl.multiple_of(i * BLOCK, BLOCK), BLOCK)
        x[rows, :] = jnp.where(
            wide4(col[rows, :]) > 0.5, tgt[rows, :].astype(F32), dec[rows, :].astype(F32)
        ).astype(BF)

    col[...] = jnp.broadcast_to(sent_f, (128, length)).T
    for i in range(blocks):
        start, wide = window(i, length)
        keys = col[pl.ds(start, wide), :]
        bias[i, pl.ds(0, wide), :] = jnp.where(
            jnp.concatenate([keys, keys], axis=1) == sent_f[:, i * BLOCK : (i + 1) * BLOCK], 0.0, -1e9
        )

    @pl.loop(0, blocks)
    def _(i):
        rows = pl.ds(pl.multiple_of(i * BLOCK, BLOCK), BLOCK)
        x_blk = x[rows, :]
        q1[rows, :] = dot(x_blk, wa1[:, :width]).astype(BF) * jnp.asarray(scale, BF)
        k1[rows, :] = dot(x_blk, wa1[:, width : 2 * width]).astype(BF)
        v = dot(x_blk, wa1[:, 2 * width :]).astype(BF)
        v1[rows, :] = v
        turn[:, rows] = v.T

    attend(q1, k1, turn, o1, lse1, bias, length)

    @pl.loop(0, blocks)
    def _(i):
        rows = pl.ds(pl.multiple_of(i * BLOCK, BLOCK), BLOCK)
        resid = x[rows, :].astype(F32) + dot(o1[rows, :], wo1[...])
        normed, inv = norm_parts(resid)
        n1[rows, :] = normed
        inv1[rows, :] = jnp.broadcast_to(inv, (BLOCK, 128))
        h1b = (normed * row(0) + row(1)).astype(BF)
        q2[rows, :] = dot(h1b, wa2[:, :width]).astype(BF) * jnp.asarray(scale, BF)
        e_blk = enc[rows, :]
        k2[rows, :] = dot(e_blk, wa2[:, width : 2 * width]).astype(BF)
        v = dot(e_blk, wa2[:, 2 * width :]).astype(BF)
        v2[rows, :] = v
        turn[:, rows] = v.T

    attend(q2, k2, turn, o2, lse2, bias, length)

    small_grad[...] = jnp.zeros_like(small_grad)
    hidden = w1.shape[1]
    step = 512
    parts = hidden // step

    def add_small(r, value):
        small_grad[pl.ds(r, 1), :] += jnp.sum(value, axis=0, keepdims=True)

    @pl.loop(0, blocks)
    def _(i):
        rows = pl.ds(pl.multiple_of(i * BLOCK, BLOCK), BLOCK)
        h1 = n1[rows, :] * row(0) + row(1)
        resid = h1 + dot(o2[rows, :], wo2[...])
        normed2, inv = norm_parts(resid)
        n2[rows, :] = normed2
        inv2[rows, :] = jnp.broadcast_to(inv, (BLOCK, 128))
        h2 = normed2 * row(2) + row(3)
        h2_low = h2.astype(BF)
        h2b[rows, :] = h2_low
        for c in range(parts):
            cols = slice(c * step, (c + 1) * step)
            u = dot(h2_low, w1[:, cols]) + small[pl.ds(7 + c, 1), :]
            act, der = gelu_pair(u)
            hid[rows, cols] = act.astype(BF)
            slope[pl.ds(c * BLOCK, BLOCK), :] = der
        resid3 = h2 + (dot(hid[rows, :], w2[...]) + row(6))
        normed3, inv3 = norm_parts(resid3)
        layer_out[rows, :] = (normed3 * row(4) + row(5)).astype(BF)
        up = og[rows, :].astype(F32)
        add_small(4, up * normed3)
        add_small(5, up)
        dr3 = norm_back(up, row(4), normed3, inv3)
        dz_low = dr3.astype(BF)
        dz[rows, :] = dz_low
        add_small(6, dz_low.astype(F32))
        for c in range(parts):
            cols = slice(c * step, (c + 1) * step)
            d = (dot_nt(dz_low, w2[cols, :]) * slope[pl.ds(c * BLOCK, BLOCK), :]).astype(BF)
            du[rows, cols] = d
            add_small(7 + c, d.astype(F32))
        dh2 = dr3 + dot_nt(du[rows, :], w1[...])
        normed2 = n2[rows, :]
        add_small(2, dh2 * normed2)
        add_small(3, dh2)
        dr2 = norm_back(dh2, row(2), normed2, wide4(inv2[rows, :]))
        in_grad[rows, :] = dr2
        da_low = dr2.astype(BF)
        da[rows, :] = da_low
        do[rows, :] = dot_nt(da_low, wo2[...]).astype(BF)

    @pl.loop(0, hidden // 256)
    def _(c):
        cols = pl.ds(pl.multiple_of(c * 256, 256), 256)
        g2[cols, :] = dot_tn(hid[:, cols], dz[...]).astype(BF)

    @pl.loop(0, width // 128)
    def _(c):
        cols = pl.ds(pl.multiple_of(c * 128, 128), 128)
        g1[cols, :] = dot_tn(h2b[:, cols], du[...]).astype(BF)
        go2[cols, :] = dot_tn(o2[:, cols], da[...]).astype(BF)

    dk, dv = slope, n2
    dqkv = hid

    turn[...] = k2[...].T
    attend_back(q2, k2, v2, turn, do, lse2, bias, dqkv, dk, dv, length)
    dqkv[:, width : 2 * width] = dk[...].astype(BF)
    dqkv[:, 2 * width : 3 * width] = dv[...].astype(BF)

    @pl.loop(0, blocks)
    def _(i):
        rows = pl.ds(pl.multiple_of(i * BLOCK, BLOCK), BLOCK)
        normed = n1[rows, :]
        h2b[rows, :] = (normed * row(0) + row(1)).astype(BF)
        dh1 = in_grad[rows, :] + dot_nt(dqkv[rows, :width], wa2[:, :width])
        add_small(0, dh1 * normed)
        add_small(1, dh1)
        dr1 = norm_back(dh1, row(0), normed, wide4(inv1[rows, :]))
        in_grad[rows, :] = dr1
        da_low = dr1.astype(BF)
        da[rows, :] = da_low
        do[rows, :] = dot_nt(da_low, wo1[...]).astype(BF)

    @pl.loop(0, width // 128)
    def _(c):
        cols = pl.ds(pl.multiple_of(c * 128, 128), 128)
        ga2[cols, :width] = dot_tn(h2b[:, cols], dqkv[:, :width]).astype(BF)
        ga2[cols, width:] = dot_tn(enc[:, cols], dqkv[:, width : 3 * width]).astype(BF)
        go1[cols, :] = dot_tn(o1[:, cols], da[...]).astype(BF)

    turn[...] = k1[...].T
    attend_back(q1, k1, v1, turn, do, lse1, bias, dqkv, dk, dv, length)
    dqkv[:, width : 2 * width] = dk[...].astype(BF)
    dqkv[:, 2 * width : 3 * width] = dv[...].astype(BF)

    @pl.loop(0, width // 128)
    def _(c):
        cols = pl.ds(pl.multiple_of(c * 128, 128), 128)
        ga1[cols, :] = dot_tn(x[:, cols], dqkv[:, : 3 * width]).astype(BF)

    @pl.loop(0, blocks)
    def _(i):
        rows = pl.ds(pl.multiple_of(i * BLOCK, BLOCK), BLOCK)
        in_grad[rows, :] += dot_nt(dqkv[rows, : 3 * width], wa1[...])


def run_layer(sid, rank, ham, dec, tgt, enc, og, wa1, wo1, wa2, wo2, w1, w2, small):
    length, width = dec.shape
    hidden = w1.shape[1]
    sds = jax.ShapeDtypeStruct
    vm = pl.BlockSpec(memory_space=pltpu.VMEM)
    tok_b = pltpu.VMEM((length, width), BF)
    tok_f = pltpu.VMEM((length, width), F32)
    return pl.pallas_call(
        layer_kernel,
        out_shape=(
            sds((length, width), BF),
            sds((length, width), F32),
            sds(w1.shape, BF), sds(w2.shape, BF), sds(wo2.shape, BF), sds(wa2.shape, BF),
            sds(wo1.shape, BF), sds(wa1.shape, BF), sds(small.shape, F32),
        ),
        in_specs=[vm, vm, pl.BlockSpec(memory_space=pltpu.SMEM)] + [vm] * 11,
        out_specs=(vm,) * 9,
        scratch_shapes=[tok_b] * 9
        + [pltpu.VMEM((width, length), BF), tok_f, tok_f]
        + [pltpu.VMEM((length, 128), F32)] * 2
        + [pltpu.VMEM((length, hidden), BF)] * 2
        + [tok_b, tok_b, tok_f, tok_b, tok_b]
        + [pltpu.VMEM((length // BLOCK, 2 * BLOCK, BLOCK), F32)]
        + [pltpu.VMEM((HEADS, length), F32)] * 2
        + [pltpu.VMEM((length, 128), F32)],
        compiler_params=pltpu.CompilerParams(vmem_limit_bytes=63 * 2**20),
        name="layer",
    )(sid, rank, ham, dec, tgt, enc, og, wa1, wo1, wa2, wo2, w1, w2, small)


def body(
    decoder_input,
    target_embed,
    encoder_states,
    sentence_ids,
    position_ranks,
    hamming_counts,
    output_grad,
    attn_in,
    attn_out,
    ffn_in,
    ffn_out,
    small_params,
    attn_in_mom,
    attn_out_mom,
    ffn_in_mom,
    ffn_out_mom,
    small_mom,
    attn_in_err,
    attn_out_err,
    ffn_in_err,
    ffn_out_err,
    attn_in_fac,
    attn_out_fac,
    ffn_in_fac,
    ffn_out_fac,
    attn_in_avg,
    attn_out_avg,
    ffn_in_avg,
    ffn_out_avg,
    small_avg,
):
    small_full = lax.all_gather(
        small_params.astype(BF), "wide", axis=1, tiled=True
    ).astype(F32)

    def columns(stack):
        return jnp.swapaxes(stack, 0, 1).reshape(stack.shape[1], -1)

    def gather(rows):
        return lax.all_gather(rows.astype(BF), "wide", axis=0, tiled=True)

    whole = [
        gather(columns(attn_in[:3])), gather(attn_out[0]),
        gather(columns(attn_in[3:])), gather(attn_out[1]),
        gather(ffn_in[0]), gather(ffn_out[0]),
    ]
    length = decoder_input.shape[1]
    layer_out, input_grad, g1, g2, go2, ga2, go1, ga1, small_grad = run_layer(
        sentence_ids, position_ranks, hamming_counts, decoder_input[0], target_embed[0],
        encoder_states[0], output_grad[0], *whole, small_full
    )

    def scatter(rows):
        return lax.psum_scatter(rows, "wide", scatter_dimension=0, tiled=True).astype(F32)

    def stack_of(rows):
        return jnp.swapaxes(rows.reshape(rows.shape[0], -1, g1.shape[0]), 0, 1)

    second, first = scatter(g2), scatter(g1)
    out_two, in_two, out_one, in_one = scatter(go2), scatter(ga2), scatter(go1), scatter(ga1)
    shards = (
        jnp.concatenate([stack_of(in_one), stack_of(in_two)], axis=0),
        jnp.stack([out_one, out_two]),
        first[None],
        second[None],
        lax.psum_scatter(small_grad, "wide", scatter_dimension=1, tiled=True),
    )
    scaling = (length * lax.axis_size("wide")) ** (-0.5)
    replicas = lax.axis_size("rep")
    fulls, lefts = ([], [])
    for gradient, error, factor_in in zip(
        shards[:4],
        (attn_in_err, attn_out_err, ffn_in_err, ffn_out_err),
        (attn_in_fac, attn_out_fac, ffn_in_fac, ffn_out_fac),
    ):
        full_grad = gradient * scaling + error[0]
        fulls.append(full_grad)
        lefts.append(jnp.einsum("knm,kmq->knq", full_grad, factor_in, precision=FULL_PRECISION))
    summed = lax.psum((lefts[0], lefts[1], lefts[2], lefts[3], shards[4] * scaling), "rep")
    left_mean = [piece / replicas for piece in summed[:4]]
    local_grams = [
        jnp.einsum("knq,kns->kqs", piece, piece, precision=FULL_PRECISION) for piece in left_mean
    ]
    grams = lax.psum((local_grams[0], local_grams[1], local_grams[2], local_grams[3]), "wide")
    orthos, rights = ([], [])
    for full_grad, piece, gram in zip(fulls, left_mean, grams):
        cholesky_factor = jnp.linalg.cholesky(gram)
        orthonormal = jnp.swapaxes(
            jax.scipy.linalg.solve_triangular(
                cholesky_factor, jnp.swapaxes(piece, 1, 2), lower=True
            ),
            1,
            2,
        )
        orthos.append(orthonormal)
        rights.append(jnp.einsum("knm,knq->kmq", full_grad, orthonormal, precision=FULL_PRECISION))
    right_sums = lax.psum((rights[0], rights[1], rights[2], rights[3]), ("rep", "wide"))
    reduced, new_errors, new_factors = ([], [], [])
    for full_grad, orthonormal, right_sum in zip(fulls, orthos, right_sums):
        right_mean = right_sum / replicas
        approx = jnp.einsum("knq,kmq->knm", orthonormal, right_mean, precision=FULL_PRECISION)
        reduced.append(approx)
        new_errors.append((full_grad - approx)[None])
        new_factors.append(right_mean)
    reduced.append(summed[4] / replicas)
    masters = (attn_in, attn_out, ffn_in, ffn_out, small_params)
    momenta = (attn_in_mom, attn_out_mom, ffn_in_mom, ffn_out_mom, small_mom)
    averages = (attn_in_avg, attn_out_avg, ffn_in_avg, ffn_out_avg, small_avg)
    rates = (LEARN_RATE, LEARN_RATE, LEARN_RATE, LEARN_RATE, VECTOR_RATE)
    new_weights, new_momenta, new_averages = ([], [], [])
    for master, moment, average, update, rate in zip(masters, momenta, averages, reduced, rates):
        moment_new = MOMENTUM * moment + update
        weight_new = master - rate * moment_new
        new_weights.append(weight_new)
        new_momenta.append(moment_new)
        new_averages.append(average + AVERAGE * (weight_new - average))
    return (
        layer_out[None],
        input_grad[None],
        new_weights[0],
        new_weights[1],
        new_weights[2],
        new_weights[3],
        new_weights[4],
        new_momenta[0],
        new_momenta[1],
        new_momenta[2],
        new_momenta[3],
        new_momenta[4],
        new_errors[0],
        new_errors[1],
        new_errors[2],
        new_errors[3],
        new_factors[0],
        new_factors[1],
        new_factors[2],
        new_factors[3],
        new_averages[0],
        new_averages[1],
        new_averages[2],
        new_averages[3],
        new_averages[4],
    )


def solution(mesh):
    placed = (
        P(("rep", "wide"), None, None),
        P(("rep", "wide"), None, None),
        P(("rep", "wide"), None, None),
        P(("rep", "wide"), None),
        P(("rep", "wide"), None),
        P(("rep", "wide"), None),
        P(("rep", "wide"), None, None),
        P(None, "wide", None),
        P(None, "wide", None),
        P(None, "wide", None),
        P(None, "wide", None),
        P(None, "wide"),
        P(None, "wide", None),
        P(None, "wide", None),
        P(None, "wide", None),
        P(None, "wide", None),
        P(None, "wide"),
        P("rep", None, "wide", None),
        P("rep", None, "wide", None),
        P("rep", None, "wide", None),
        P("rep", None, "wide", None),
        P(),
        P(),
        P(),
        P(),
        P(None, "wide", None),
        P(None, "wide", None),
        P(None, "wide", None),
        P(None, "wide", None),
        P(None, "wide"),
    )
    return jax.shard_map(
        body,
        mesh=mesh,
        in_specs=placed,
        out_specs=(
            P(("rep", "wide"), None, None),
            P(("rep", "wide"), None, None),
            P(None, "wide", None),
            P(None, "wide", None),
            P(None, "wide", None),
            P(None, "wide", None),
            P(None, "wide"),
            P(None, "wide", None),
            P(None, "wide", None),
            P(None, "wide", None),
            P(None, "wide", None),
            P(None, "wide"),
            P("rep", None, "wide", None),
            P("rep", None, "wide", None),
            P("rep", None, "wide", None),
            P("rep", None, "wide", None),
            P(),
            P(),
            P(),
            P(),
            P(None, "wide", None),
            P(None, "wide", None),
            P(None, "wide", None),
            P(None, "wide", None),
            P(None, "wide"),
        ),
        check_vma=False,
    )
```

```python
import functools
import types

import jax
import jax.numpy as jnp
from jax import lax
from jax.experimental import pallas as pl
from jax.experimental.pallas import tpu as pltpu
from jax.sharding import PartitionSpec as P

HEADS = 8
HEAD_DIM = 64
RANK = 8
BLOCK = 256
SPAN = 128
TOGETHER = 2
EPS = 1e-05
FAR = -(2.0**30)
BF = jnp.bfloat16
F32 = jnp.float32
FULL_PRECISION = lax.Precision.HIGHEST
MOMENTUM = 0.9
LEARN_RATE = 0.1
VECTOR_RATE = 0.5
AVERAGE = 0.25
MESH = pl.DeviceIdType.MESH
VMEM_BYTES = 64 * 2**20 - 2**16

A1, O1, A2, O2, W1, W2 = range(6)


def dot(a, b, precision=None):
    return lax.dot_general(
        a, b, (((1,), (0,)), ((), ())), precision=precision, preferred_element_type=F32
    )


def dot_nt(a, b, precision=None):
    return lax.dot_general(
        a, b, (((1,), (1,)), ((), ())), precision=precision, preferred_element_type=F32
    )


def dot_tn(a, b, precision=None):
    return lax.dot_general(
        a, b, (((0,), (0,)), ((), ())), precision=precision, preferred_element_type=F32
    )


def gelu_pair(u):
    half = 0.5 * (1.0 + lax.erf(u * 0.7071067811865476))
    return u * half, half + u * jnp.exp(-0.5 * u * u) * 0.3989422804014327


def wide4(col):
    return jnp.concatenate([col] * 4, axis=1)


def norm_parts(resid):
    center = resid - jnp.mean(resid, axis=-1, keepdims=True)
    inv = lax.rsqrt(jnp.mean(center * center, axis=-1, keepdims=True) + EPS)
    return center * inv, inv


def norm_back(up, gain, normed, inv):
    scaled = up * gain
    return inv * (
        scaled
        - jnp.mean(scaled, axis=-1, keepdims=True)
        - normed * jnp.mean(scaled * normed, axis=-1, keepdims=True)
    )


def split_heads(pair):
    first = lax.broadcasted_iota(jnp.int32, pair.shape, 1) < HEAD_DIM
    zero = jnp.zeros_like(pair)
    return jnp.concatenate([jnp.where(first, pair, zero), jnp.where(first, zero, pair)], axis=0)


def join_heads(value):
    return jnp.concatenate(
        [value[:HEAD_DIM, :SPAN], value[HEAD_DIM:, SPAN:]], axis=0
    ).T


PAIRS = [pl.ds(128 * pair, 128) for pair in range(HEADS // 2)]


def spans(length):
    for i in range(length // SPAN):
        start, end = max(0, (i - 1) * SPAN), min(length, (i + 2) * SPAN)
        yield i, pl.ds(i * SPAN, SPAN), pl.ds(start, end - start)


def scores(b, q_both, k, rows, keys):
    near = b.near_q[rows, :]
    near = jnp.concatenate([near, near], axis=0)
    far = b.far_k[keys, :]
    return [
        dot_nt(jnp.concatenate([k[keys, p], far], axis=1), jnp.concatenate([both, near], axis=1))
        for p, both in zip(PAIRS, q_both)
    ]


def attend(b, q, k, v_t, o, lse, hook):
    for i, rows, keys in spans(q.shape[0]):
        s = scores(b, [split_heads(q[rows, p]) for p in PAIRS], k, rows, keys)
        peak = [jnp.max(one, axis=0, keepdims=True) for one in s]
        e = [jnp.exp(one - top) for one, top in zip(s, peak)]
        total = [jnp.sum(one, axis=0, keepdims=True) for one in e]
        prob = [(one * (1.0 / norm)).astype(BF) for one, norm in zip(e, total)]
        mixed = [dot(v_t[p, keys], one) for p, one in zip(PAIRS, prob)]
        for n, p in enumerate(PAIRS):
            lse[i * len(PAIRS) + n] = peak[n] + jnp.log(total[n])
            o[rows, p] = join_heads(mixed[n]).astype(BF)
        if i % 2:
            hook(i // 2)


def attend_back(b, q, k, v, k_t, do, lse, dqkv, sums, hook):
    length, width = q.shape
    last = length // SPAN - 1
    for i, rows, keys in spans(length):
        q_both = [split_heads(q[rows, p]) for p in PAIRS]
        d_both = [split_heads(do[rows, p]) for p in PAIRS]
        s = scores(b, q_both, k, rows, keys)
        dp = [dot_nt(v[keys, p], both) for p, both in zip(PAIRS, d_both)]
        prob = [jnp.exp(one - lse[i * len(PAIRS) + n]) for n, one in enumerate(s)]
        diag = [jnp.sum(x * y, axis=0, keepdims=True) for x, y in zip(prob, dp)]
        ds = [(x * (y - z)).astype(BF) for x, y, z in zip(prob, dp, diag)]
        low = [x.astype(BF) for x in prob]
        for n, p in enumerate(PAIRS):
            parts = (dot(ds[n], q_both[n]), dot(low[n], d_both[n]))
            for m, j in enumerate(range(max(0, i - 1), min(last, i + 1) + 1)):
                for which, part in enumerate(parts):
                    at = (pl.ds((3 * which + j % 3) * SPAN, SPAN), p)
                    piece = part[m * SPAN : (m + 1) * SPAN]
                    if i == max(0, j - 1):
                        sums[at] = piece
                    else:
                        sums[at] += piece
        dq_t = [dot(k_t[p, keys], one) for p, one in zip(PAIRS, ds)]
        for n, p in enumerate(PAIRS):
            dqkv[rows, p] = (join_heads(dq_t[n]) * HEAD_DIM ** (-0.5)).astype(BF)
        for j in [i - 1] * (i > 0) + [i] * (i == last):
            for which in range(2):
                done = sums[pl.ds((3 * which + j % 3) * SPAN, SPAN), :]
                dqkv[pl.ds(j * SPAN, SPAN), pl.ds((1 + which) * width, width)] = done.astype(BF)
        if i % 2:
            hook(i // 2)


def flat(ref, *at):
    value = ref[at] if at else ref[...]
    return value.reshape(-1, value.shape[-1])


def columns_of(ref, first, count):
    return flat(ref, *(slice(None),) * (len(ref.shape) - 1), pl.ds(first, count))


def layer_math(b, hook):
    w, g = b.weights, b.grads
    length, width = b.x.shape
    blocks = length // BLOCK
    chips = w[A1].shape[0]
    hidden = w[W1].shape[-1]
    parts = hidden // 512
    scale = jnp.asarray(HEAD_DIM ** (-0.5), BF)
    row = lambda r: b.small[pl.ds(r, 1), :]

    def each_block(body):
        for i in range(blocks):
            body(pl.ds(i * BLOCK, BLOCK))

    sent = b.sid[...]
    per_pos = jnp.zeros_like(sent)
    for s in range(b.ham.shape[1]):
        per_pos = jnp.where(sent == s, b.ham[0, s], per_pos)
    glance = jnp.where(2 * b.rank[...] < per_pos, 1.0, 0.0).astype(F32)
    sent_f = sent.astype(F32)
    b.col[...] = jnp.broadcast_to(glance, (128, length)).T
    hook("inputs")

    @each_block
    def _(rows):
        b.x[rows, :] = jnp.where(
            wide4(b.col[rows, :]) > 0.5, b.da[rows, :].astype(F32), b.x[rows, :].astype(F32)
        ).astype(BF)

    hook("mixed")
    b.col[...] = jnp.broadcast_to(sent_f, (128, length)).T

    @each_block
    def _(rows):
        here = b.col[rows, :]
        same = lax.broadcasted_iota(jnp.int32, here.shape, 1).astype(F32) == here
        b.near_q[rows, :] = jnp.where(same, 1.0, 0.0).astype(BF)
        b.far_k[rows, :] = jnp.where(same, 0.0, FAR).astype(BF)

    hook("masked")

    @each_block
    def _(rows):
        x_blk = b.x[rows, :]
        b.q1[rows, :] = dot(x_blk, columns_of(w[A1], 0, width)).astype(BF) * scale
        b.k1[rows, :] = dot(x_blk, columns_of(w[A1], width, width)).astype(BF)
        v = dot(x_blk, columns_of(w[A1], 2 * width, width)).astype(BF)
        b.v1[rows, :] = v
        b.turn[:, rows] = v.T

    hook("qkv1")
    attend(b, b.q1, b.k1, b.turn, b.o1, b.lse1, lambda i: hook(("attend1", i)))
    hook("need_small")
    hook(("need", O1))
    hook(("need", A2))

    @each_block
    def _(rows):
        resid = b.x[rows, :].astype(F32) + dot(b.o1[rows, :], flat(w[O1]))
        normed, inv = norm_parts(resid)
        b.n1[rows, :] = normed
        b.col[rows, :] = jnp.broadcast_to(inv, (BLOCK, 128))
        h1b = (normed * row(0) + row(1)).astype(BF)
        b.q2[rows, :] = dot(h1b, columns_of(w[A2], 0, width)).astype(BF) * scale
        e_blk = b.enc[rows, :]
        b.k2[rows, :] = dot(e_blk, columns_of(w[A2], width, width)).astype(BF)
        v = dot(e_blk, columns_of(w[A2], 2 * width, width)).astype(BF)
        b.v2[rows, :] = v
        b.turn[:, rows] = v.T

    hook("qkv2")
    attend(b, b.q2, b.k2, b.turn, b.o2, b.lse2, lambda i: hook(("attend2", i)))
    hook(("need", O2))
    hook(("need", W1))

    b.small_grad[...] = jnp.zeros_like(b.small_grad)

    def add_small(r, value):
        b.small_grad[pl.ds(r, 1), :] += jnp.sum(value, axis=0, keepdims=True)

    per = hidden // chips
    chunk = [pl.ds(c * 512, 512) for c in range(parts)]
    for first in range(0, blocks, TOGETHER):
        group = [pl.ds((first + n) * BLOCK, BLOCK) for n in range(TOGETHER)]
        h1 = [b.n1[rows, :] * row(0) + row(1) for rows in group]
        resid = [h + dot(b.o2[rows, :], flat(w[O2])) for h, rows in zip(h1, group)]
        normed2, inv2 = zip(*[norm_parts(r) for r in resid])
        h2 = [n * row(2) + row(3) for n in normed2]
        h2_low = [h.astype(BF) for h in h2]
        for n, rows in enumerate(group):
            b.n2[pl.ds(n * BLOCK, BLOCK), :] = normed2[n]
            b.inv2[pl.ds(n * BLOCK, BLOCK), :] = jnp.broadcast_to(inv2[n], (BLOCK, 128))
            b.h2b[rows, :] = h2_low[n]
        for c in range(parts):
            us = [dot(h, columns_of(w[W1], c * 512, 512)) + row(7 + c) for h in h2_low]
            for n, rows in enumerate(group):
                act, der = gelu_pair(us[n])
                b.hid[rows, chunk[c]] = act.astype(BF)
                b.slope[pl.ds((n * parts + c) * BLOCK, BLOCK), :] = der
        if first == 0:
            hook("gelu")
            hook(("need", W2))
        resid3 = [
            h + (dot(b.hid[rows, :], flat(w[W2])) + row(6)) for h, rows in zip(h2, group)
        ]
        normed3, inv3 = zip(*[norm_parts(r) for r in resid3])
        ups = [b.og[rows, :].astype(F32) for rows in group]
        dr3 = [norm_back(up, row(4), n, i) for up, n, i in zip(ups, normed3, inv3)]
        dz_low = [d.astype(BF) for d in dr3]
        for n, rows in enumerate(group):
            b.og[rows, :] = (normed3[n] * row(4) + row(5)).astype(BF)
            add_small(4, ups[n] * normed3[n])
            add_small(5, ups[n])
            b.dz[rows, :] = dz_low[n]
            add_small(6, dz_low[n].astype(F32))
        for c in range(chips):
            ds = [dot_nt(d, flat(w[W2], c)) for d in dz_low]
            for half in range(per // 512):
                at = c * (per // 512) + half
                for n, rows in enumerate(group):
                    part = ds[n][:, half * 512 : (half + 1) * 512]
                    low = (part * b.slope[pl.ds((n * parts + at) * BLOCK, BLOCK), :]).astype(BF)
                    b.du[rows, chunk[at]] = low
                    add_small(7 + at, low.astype(F32))
        dh2 = [d + dot_nt(b.du[rows, :], flat(w[W1])) for d, rows in zip(dr3, group)]
        normed2 = [b.n2[pl.ds(n * BLOCK, BLOCK), :] for n in range(TOGETHER)]
        inv2 = [b.inv2[pl.ds(n * BLOCK, BLOCK), :] for n in range(TOGETHER)]
        dr2 = [norm_back(d, row(2), n, wide4(i)) for d, n, i in zip(dh2, normed2, inv2)]
        da_low = [d.astype(BF) for d in dr2]
        do = [dot_nt(d, flat(w[O2])).astype(BF) for d in da_low]
        for n, rows in enumerate(group):
            add_small(2, dh2[n] * normed2[n])
            add_small(3, dh2[n])
            b.in_grad[rows, :] = dr2[n]
            b.da[rows, :] = da_low[n]
            b.do[rows, :] = do[n]

    hook("layer_out")

    for c in range(2 * chips):
        rows = hidden // (2 * chips)
        cols = pl.ds(c * rows, rows)
        g[W2][c // 2, c % 2] = dot_tn(b.hid[:, cols], b.dz[...]).astype(BF)

    hook(("grad", W2))

    def each_chip(body):
        per = width // chips
        for c in range(chips):
            body(c, pl.ds(c * per, per))

    def put(ref, c, first, value):
        shape = (2, value.shape[0] // 2, value.shape[1])
        ref[c, :, :, pl.ds(first, value.shape[1])] = value.astype(BF).reshape(shape)

    @each_chip
    def _(c, cols):
        put(g[W1], c, 0, dot_tn(b.h2b[:, cols], b.du[...]))

    hook(("grad", W1))

    @each_chip
    def _(c, cols):
        put(g[O2], c, 0, dot_tn(b.o2[:, cols], b.da[...]))

    hook(("grad", O2))

    dqkv = b.hid
    q_part, kv_part, all_part = pl.ds(0, width), pl.ds(width, 2 * width), pl.ds(0, 3 * width)

    def turn_keys(keys):
        @each_block
        def _(rows):
            b.turn[:, rows] = keys[rows, :].T

    turn_keys(b.k2)
    attend_back(
        b, b.q2, b.k2, b.v2, b.turn, b.do, b.lse2, dqkv, b.slope, lambda i: hook(("back2", i))
    )

    @each_block
    def _(rows):
        normed = b.n1[rows, :]
        b.h2b[rows, :] = (normed * row(0) + row(1)).astype(BF)
        dh1 = b.in_grad[rows, :] + dot_nt(dqkv[rows, q_part], columns_of(w[A2], 0, width))
        add_small(0, dh1 * normed)
        add_small(1, dh1)
        dr1 = norm_back(dh1, row(0), normed, wide4(b.col[rows, :]))
        b.in_grad[rows, :] = dr1
        da_low = dr1.astype(BF)
        b.da[rows, :] = da_low
        b.do[rows, :] = dot_nt(da_low, flat(w[O1])).astype(BF)

    hook("norm1")

    @each_chip
    def _(c, cols):
        put(g[A2], c, 0, dot_tn(b.h2b[:, cols], dqkv[:, q_part]))
        put(g[A2], c, width, dot_tn(b.enc[:, cols], dqkv[:, kv_part]))

    hook(("grad", A2))

    @each_chip
    def _(c, cols):
        put(g[O1], c, 0, dot_tn(b.o1[:, cols], b.da[...]))

    hook(("grad", O1))
    turn_keys(b.k1)
    attend_back(
        b, b.q1, b.k1, b.v1, b.turn, b.do, b.lse1, dqkv, b.slope, lambda i: hook(("back1", i))
    )

    @each_chip
    def _(c, cols):
        put(g[A1], c, 0, dot_tn(b.x[:, cols], dqkv[:, all_part]))

    hook(("grad", A1))

    @each_block
    def _(rows):
        b.in_grad[rows, :] += dot_nt(dqkv[rows, all_part], flat(w[A1]))

    hook("in_grad")


def math_scratch(length, width, hidden, small_rows):
    low, full = pltpu.VMEM((length, width), BF), pltpu.VMEM((length, width), F32)
    totals = pltpu.VMEM((length // SPAN * len(PAIRS), 1, 2 * SPAN), F32)
    marks = pltpu.VMEM((length, 128), BF)
    return dict(
        x=low, enc=low, og=low, q1=low, k1=low, v1=low, o1=low, q2=low, k2=low, v2=low, o2=low,
        turn=pltpu.VMEM((width, length), BF),
        n1=full, n2=pltpu.VMEM((TOGETHER * BLOCK, width), F32),
        inv2=pltpu.VMEM((TOGETHER * BLOCK, 128), F32),
        hid=pltpu.VMEM((length, hidden), BF), du=pltpu.VMEM((length, hidden), BF),
        dz=low, h2b=low, slope=pltpu.VMEM((TOGETHER * length, width), F32), in_grad=full, da=low, do=low,
        lse1=totals, lse2=totals, near_q=marks, far_k=marks,
        col=pltpu.VMEM((length, 128), F32),
        small_grad=pltpu.VMEM((small_rows, width), F32),
    )


def half_of(core, pair):
    return jnp.where(core == 0, pair[:, :64], pair[:, 64:])


def placed(core, part):
    zero = jnp.zeros_like(part)
    return jnp.where(
        core == 0, jnp.concatenate([part, zero], axis=1), jnp.concatenate([zero, part], axis=1)
    )


def split3(value):
    high = value.astype(BF).astype(F32)
    middle = (value - high).astype(BF).astype(F32)
    low = (value - high) - middle
    return jnp.concatenate([high, middle, low, jnp.zeros_like(value)], axis=0).astype(BF)


def add3(value):
    return value[:RANK] + value[RANK : 2 * RANK] + value[2 * RANK : 3 * RANK]


def orthonormal(rows_of, count):
    single = rows_of[: count * RANK].reshape(count, RANK, -1)
    rest = rows_of[count * RANK :].reshape(-1, RANK, rows_of.shape[1])
    joined = jnp.concatenate([rest[i] for i in range(rest.shape[0])], axis=1)[None]
    done = []
    for value in (single, joined):
        index = lax.broadcasted_iota(jnp.int32, value.shape, 1)
        for j in range(RANK):
            pivot = value[:, j : j + 1, :]
            unit = pivot / jnp.sqrt(jnp.sum(pivot * pivot, axis=-1, keepdims=True))
            along = jnp.sum(value * unit, axis=-1, keepdims=True)
            value = jnp.where(index < j, value, jnp.where(index == j, unit, value - along * unit))
        done.append(value)
    width = rows_of.shape[1]
    tail = [done[1][0, :, i * width : (i + 1) * width] for i in range(rest.shape[0])]
    return jnp.concatenate([done[0].reshape(count * RANK, width)] + tail, axis=0)


def step_kernel(chips, *refs):
    b = types.SimpleNamespace()
    (b.sid, b.rank, b.ham, b.dec, b.tgt, b.enc_in, b.og_in, b.attn_in, b.attn_out, b.ffn_in, b.ffn_out,
     b.small_in, b.err_ai, b.err_ao, b.err_fi, b.err_fo, b.fac_ai, b.fac_ao, b.fac_fi, b.fac_fo,
     b.layer_out, b.in_grad_out, b.total_out, b.own_out, b.right_out, b.small_out) = refs[:26]
    refs = refs[26:]
    for key, ref in zip(SCRATCH, refs):
        setattr(b, key, ref)
    refs = refs[len(SCRATCH) :]
    weights, grads, pair_in, land = (refs[n : n + 6] for n in (0, 6, 12, 18))
    (small, small_tile, small_land, fac3, err_left, left, left_out,
     right, right_out, inbox, load_sem, ag_send, ag_recv, cc_send, cc_recv, rs_send, rs_recv,
     ar_send, ar_recv, sm_send, sm_recv, out_sem) = refs[24:]
    b.weights, b.grads, b.small = weights, grads, small
    rep, wide = lax.axis_index("rep"), lax.axis_index("wide")
    core, z = wide % 2, wide // 2
    width = b.x.shape[1]
    slots = fac3.shape[0]
    singles = 9
    sibling = (rep, wide + 1 - 2 * core)
    beside = [(rep + 1 - 2 * (rep % 2), wide), ((rep + 2) % 4, wide), (3 - rep, wide)]
    ahead = [(z + k) % chips for k in range(1, chips)]
    behind = [(z + chips - k) % chips for k in range(1, chips)]
    along = [(rep, there * 2 + core) for there in ahead]

    def remote(src, dst, send, recv, to):
        return pltpu.make_async_remote_copy(
            src_ref=src, dst_ref=dst, send_sem=send, recv_sem=recv, device_id=to, device_id_type=MESH
        )

    master, error = b.in_grad, b.slope
    loads = []

    def load(src, dst):
        copy = pltpu.make_async_copy(src, dst, load_sem.at[len(loads)])
        copy.start()
        loads.append(copy)
        return copy

    def load_state(attn_i, attn_o, ffn_i, ffn_o, to):
        rows, found = [], []
        for s in range(6):
            found.append(load(attn_i.at[s], to.at[pl.ds(64 * s, 64)]))
        for s in range(2):
            found.append(load(attn_o.at[s], to.at[pl.ds(384 + 64 * s, 64)]))
        for c in range(4):
            found.append(
                load(ffn_i.at[0, :, pl.ds(c * width, width)], to.at[pl.ds(512 + 64 * c, 64)])
            )
        found.append(load(ffn_o.at[0], to.at[pl.ds(768, 256)]))
        return found

    masters = load_state(b.attn_in, b.attn_out, b.ffn_in, b.ffn_out, master)
    acts = [load(b.dec, b.x), load(b.tgt, b.da), load(b.enc_in, b.enc), load(b.og_in, b.og)]
    errors = load_state(b.err_ai, b.err_ao, b.err_fi, b.err_fo, error)

    barrier = pltpu.get_barrier_semaphore()
    partners = [sibling] + beside + along
    for partner in partners:
        pl.semaphore_signal(barrier, inc=1, device_id=partner, device_id_type=MESH)

    def ag_along(g, k):
        ref = weights[g].at[z, core, rep]
        return remote(ref, ref, ag_send.at[g, k, 0], ag_recv.at[g, k, 0], along[k])

    def ag_along_in(g, k):
        ref = weights[g].at[behind[k], core, rep]
        return remote(ref, ref, ag_send.at[g, k, 0], ag_recv.at[g, k, 0], along[k])

    def ag_beside(g, k, j):
        ref = weights[g].at[behind[k], core, rep]
        return remote(ref, ref, ag_send.at[g, k, 1 + j], ag_recv.at[g, k, 1 + j], beside[j])

    def ag_beside_in(g, k, j):
        ref = weights[g].at[behind[k], core, beside[j][0]]
        return remote(ref, ref, ag_send.at[g, k, 1 + j], ag_recv.at[g, k, 1 + j], beside[j])

    def ag_core(g, k):
        ref = weights[g].at[z if k == 0 else behind[k - 1], core]
        return remote(ref, ref, cc_send.at[g, k], cc_recv.at[g, k], sibling)

    def ag_core_in(g, k):
        ref = weights[g].at[z if k == 0 else behind[k - 1], 1 - core]
        return remote(ref, ref, cc_send.at[g, k], cc_recv.at[g, k], sibling)

    hops = range(chips - 1)

    def own_shard(g):
        quarter = weights[g].shape[3]

        def put(at, first, count):
            value = master[pl.ds(at, 4 * quarter), :].astype(BF)
            weights[g][z, core, :, :, pl.ds(first, count)] = value.reshape(4, quarter, count)

        if g in (A1, A2):
            for s in range(3):
                put(64 * (s + (3 if g == A2 else 0)), s * width, width)
        elif g in (O1, O2):
            put(384 + (64 if g == O2 else 0), 0, width)
        elif g == W1:
            for c in range(4):
                put(512 + 64 * c, c * width, width)
        else:
            put(768, 0, width)

    def ag_start(g):
        for k in hops:
            ag_along(g, k).start()
        ag_core(g, 0).start()

    def ag_forward(g):
        for k in hops:
            ag_along_in(g, k).wait_recv()
            for j in range(3):
                ag_beside(g, k, j).start()

    def ag_cross(g):
        for k in hops:
            for j in range(3):
                ag_beside_in(g, k, j).wait_recv()
            ag_core(g, k + 1).start()

    def ag_ready(g):
        for k in range(chips):
            ag_core_in(g, k).wait_recv()

    def small_along(k):
        return remote(small_tile, small_land.at[k], sm_send.at[k], sm_recv.at[k], along[k])

    small_core = remote(small_tile, small_land.at[chips - 1], sm_send.at[chips - 1], sm_recv.at[chips - 1], sibling)

    def small_start():
        rows = small_tile.shape[0] - b.small_in.shape[0]
        value = jnp.concatenate([b.small_in[...], jnp.zeros((rows, 64), F32)], axis=0)
        small_tile[...] = placed(core, value).astype(BF)
        small_core.start()

    def small_forward():
        small_core.wait_recv()
        small_core.wait_send()
        both = small_tile[...].astype(F32) + small_land[chips - 1].astype(F32)
        small_tile[...] = both.astype(BF)
        small[:, pl.ds(pl.multiple_of(z * 128, 128), 128)] = both
        for k in hops:
            small_along(k).start()

    def small_ready():
        for k in hops:
            small_along(k).wait_recv()
            small[:, pl.ds(pl.multiple_of(behind[k] * 128, 128), 128)] = small_land[k].astype(F32)

    def rs_pair(g):
        return remote(
            grads[g].at[:, 1 - core], pair_in[g], rs_send.at[g, 0], rs_recv.at[g, 0], sibling
        )

    def rs_ring(g, s):
        chunk = (z + chips - 1 - s) % chips
        return remote(
            pair_in[g].at[chunk], land[g].at[s], rs_send.at[g, 1 + s], rs_recv.at[g, 1 + s], along[0]
        )

    def rs_start(g):
        rs_pair(g).start()

    def rs_add(g):
        rs_pair(g).wait_recv()
        for s in range(chips):
            chunk = (z + chips - 1 - s) % chips
            total = pair_in[g][chunk].astype(F32) + grads[g][chunk, core].astype(F32)
            pair_in[g][chunk] = total.astype(BF)
            if s == 0:
                rs_ring(g, 0).start()

    def rs_step(g, s):
        rs_ring(g, s).wait_recv()
        chunk = (z + 2 * chips - 2 - s) % chips
        total = land[g][s].astype(F32) + pair_in[g][chunk].astype(F32)
        pair_in[g][chunk] = total.astype(BF)
        rs_ring(g, s + 1).start()

    total = b.n1

    def rs_finish(g):
        rs_ring(g, chips - 2).wait_recv()
        value = (land[g][chips - 2].astype(F32) + pair_in[g][z].astype(F32)) * scaling
        if g in (A1, A2):
            for s in range(3):
                total[pl.ds(64 * (s + (3 if g == A2 else 0)), 64), :] = value[:, s * width : (s + 1) * width]
        elif g in (O1, O2):
            total[pl.ds(384 + (64 if g == O2 else 0), 64), :] = value
        elif g == W1:
            for c in range(4):
                total[pl.ds(512 + 64 * c, 64), :] = value[:, c * width : (c + 1) * width]
        else:
            total[pl.ds(768, 256), :] = value

    length = b.x.shape[0]
    scaling = (length * 2 * chips) ** (-0.5)

    def all_reduce(which, source, result, inbox):
        rows = lambda start, count: pl.ds(pl.multiple_of(start, 16), count)
        half = lambda c: rows(c * 64, 64)
        part = lambda r: rows(core * 64 + r * 16, 16)
        mine = part(rep)
        move = lambda src, dst, n, to: remote(src, dst, ar_send.at[which, n], ar_recv.at[which, n], to)
        fold = move(source.at[half(1 - core)], inbox.at[pl.ds(0, 64)], 0, sibling)
        over = [
            move(source.at[part(beside[j][0])], inbox.at[pl.ds(64 + 16 * j, 16)], 1 + j, beside[j])
            for j in range(3)
        ]
        up = [
            move(source.at[mine], inbox.at[pl.ds(112 + 16 * k, 16)], 4 + k, along[k]) for k in hops
        ]
        first = 3 + chips
        back = [move(result.at[mine], result.at[mine], first + j, beside[j]) for j in range(3)]
        back_in = [
            move(result.at[part(beside[j][0])], result.at[part(beside[j][0])], first + j, beside[j])
            for j in range(3)
        ]
        share = move(result.at[half(core)], result.at[half(core)], first + 3, sibling)
        share_in = move(result.at[half(1 - core)], result.at[half(1 - core)], first + 3, sibling)

        def folded():
            fold.wait_recv()
            source[half(core), :] += inbox[pl.ds(0, 64), :]
            for copy in over:
                copy.start()

        def summed():
            for copy in over:
                copy.wait_recv()
            source[mine, :] += (inbox[pl.ds(64, 16), :] + inbox[pl.ds(80, 16), :]) + inbox[pl.ds(96, 16), :]
            for copy in up:
                copy.start()

        def whole():
            for copy in up:
                copy.wait_recv()
            value = None
            for there in range(chips):
                term = source[mine, :]
                for k in hops:
                    term = jnp.where(behind[k] == there, inbox[pl.ds(112 + 16 * k, 16), :], term)
                value = term if value is None else value + term
            result[mine, :] = value
            for copy in back:
                copy.start()

        def shared():
            for copy in back_in:
                copy.wait_recv()
            share.start()

        def finish():
            for copy in [fold, share] + over + up + back:
                copy.wait_send()

        return [fold.start, folded, summed, whole, shared, share_in.wait_recv], finish

    def error_left():
        for copy in errors:
            copy.wait()
        factor = lambda s: b.fac_ai[s] if s < 6 else b.fac_ao[s - 6] if s < 8 else (
            b.fac_fi[0, :, (s - 8) * width : (s - 7) * width] if s < 12 else b.fac_fo[0]
        )
        for s in range(slots):
            fac3[s] = split3(factor(s))
        piece = lambda at: error[pl.ds(at, 64), :]
        for s in range(slots):
            if s < 8:
                value = dot_nt(factor(s), piece(64 * s), FULL_PRECISION)
            elif s == 8:
                value = sum(dot_nt(factor(8 + c), piece(512 + 64 * c), FULL_PRECISION) for c in range(4))
            else:
                value = dot_nt(factor(12), piece(768 + 64 * (s - 9)), FULL_PRECISION)
            err_left[pl.ds(s * RANK, RANK), :] = value

    def grad_of(s):
        if s < 6:
            return [(columns_of(grads[A1 if s < 3 else A2], (s % 3) * width, width), s)]
        if s < 8:
            return [(flat(grads[O1 if s == 6 else O2]), s)]
        if s == 8:
            return [(columns_of(grads[W1], c * width, width), 8 + c) for c in range(4)]
        j = s - 9
        return [(flat(grads[W2], slice(None), slice(None), pl.ds(64 * j, 64)), 12)]

    def left_of(which):
        for s in which:
            value = None
            for matrix, f in grad_of(s):
                one = dot_nt(fac3[f], matrix)
                value = one if value is None else value + one
            left[pl.ds(s * RANK, RANK), :] = add3(value) * scaling

    def left_close():
        lanes = pl.ds(pl.multiple_of(z * 128, 128), 128)
        left[pl.ds(0, slots * RANK), lanes] += placed(core, err_left[...])
        left[pl.ds(slots * RANK, 16), :] = b.small_grad[...] * scaling
        left[pl.ds(slots * RANK + 16, 8), :] = jnp.zeros((8, width), F32)

    def right_of(ph):
        own = half_of(core, left[pl.ds(0, slots * RANK), pl.ds(pl.multiple_of(z * 128, 128), 128)])
        b.own_out[...] = own
        terms = [split3(ph[s * RANK : (s + 1) * RANK]) for s in range(slots)]
        piece = lambda at: error[pl.ds(at, 64), :]
        own_of = lambda s: own[s * RANK : (s + 1) * RANK]
        values = [None] * slots
        for s in range(slots):
            for matrix, f in grad_of(s):
                one = dot(terms[s], matrix)
                values[f] = one if values[f] is None else values[f] + one
        for f in range(slots):
            value = add3(values[f]) * scaling
            if f < 8:
                value += dot(own_of(f), piece(64 * f), FULL_PRECISION)
            elif f < 12:
                value += dot(own_of(8), piece(512 + 64 * (f - 8)), FULL_PRECISION)
            else:
                for j in range(4):
                    value += dot(own_of(9 + j), piece(768 + 64 * j), FULL_PRECISION)
            right[pl.ds(f * RANK, RANK), :] = value
        right[pl.ds(slots * RANK, 24), :] = jnp.zeros((24, width), F32)

    def prepare(g, needed):
        for n in needed:
            masters[n].wait()
        own_shard(g)

    prepare(A1, (0, 1, 2))
    pl.semaphore_wait(barrier, len(partners))
    ag_start(A1)
    prepare(O1, (6,))
    ag_start(O1)
    small_start()
    reduce_left, close_left = all_reduce(0, left, left_out, inbox.at[0])
    reduce_right, close_right = all_reduce(1, right, right_out, inbox.at[1])

    def wait_loads(which):
        for copy in which:
            copy.wait()

    reload = []

    def reload_errors():
        reload.extend(load_state(b.err_ai, b.err_ao, b.err_fi, b.err_fo, error))

    def out_copy(src, dst, i):
        return pltpu.make_async_copy(src, dst, out_sem.at[i])

    outs = [out_copy(b.og, b.layer_out, 0), out_copy(b.in_grad, b.in_grad_out, 1), out_copy(total, b.total_out, 2)]
    plan = {
        "inputs": [lambda: wait_loads(acts[:2])],
        "mixed": [
            lambda: prepare(A2, (3, 4, 5)), lambda: prepare(O2, (7,)), lambda: ag_forward(A1),
            lambda: ag_start(A2),
        ],
        "masked": [
            small_forward, lambda: ag_forward(O1), lambda: ag_start(O2),
            lambda: prepare(W1, (8, 9, 10, 11)), lambda: prepare(W2, (12,)), lambda: ag_start(W1),
            lambda: ag_cross(A1), error_left, lambda: ag_forward(A2), lambda: ag_start(W2),
            lambda: ag_ready(A1),
        ],
        "qkv1": [lambda: ag_cross(O1), lambda: ag_forward(O2)],
        ("attend1", 1): [lambda: ag_forward(W1)],
        ("attend1", 3): [lambda: ag_cross(A2)],
        "need_small": [small_ready, lambda: wait_loads(acts[2:])],
        "qkv2": [lambda: ag_cross(O2), lambda: ag_forward(W2)],
        ("attend2", 3): [lambda: ag_cross(W1)],
        "gelu": [lambda: ag_cross(W2)],
        "layer_out": [outs[0].start],
        ("grad", W2): [lambda: rs_start(W2)],
        ("grad", W1): [lambda: rs_add(W2), lambda: rs_start(W1)],
        ("grad", O2): [lambda: rs_start(O2)],
        ("back2", 0): [lambda: rs_add(W1), lambda: rs_add(O2)],
        ("back2", 3): [lambda: rs_step(W2, 0)],
        ("grad", A2): [lambda: rs_start(A2)],
        ("grad", O1): [
            lambda: rs_start(O1), lambda: left_of((8, 9, 10, 11, 12, 7)), lambda: rs_step(W1, 0),
        ],
        ("back1", 0): [lambda: rs_add(A2), lambda: rs_add(O1)],
        ("back1", 1): [lambda: rs_step(O2, 0), lambda: left_of((3, 4, 5, 6))],
        ("back1", 2): [lambda: rs_step(W2, 1)],
        ("grad", A1): [
            lambda: rs_start(A1), lambda: left_of((0, 1, 2)), left_close, reduce_left[0],
            reload_errors,
        ],
        "in_grad": [outs[1].start],
    }
    for g in (O1, A2, O2, W1, W2):
        plan[("need", g)] = [lambda g=g: ag_ready(g)]

    def hook(name):
        for action in plan.pop(name, ()):
            action()

    layer_math(b, hook)

    reduce_left[1]()
    rs_step(W1, 1)
    rs_add(A1)
    reduce_left[2]()
    rs_step(O2, 1)
    rs_step(A2, 0)
    rs_step(O1, 0)
    for step in reduce_left[3:]:
        step()
    close_left()
    rs_finish(W2)
    ph = orthonormal(left_out[pl.ds(0, slots * RANK), :], singles)
    left[pl.ds(0, slots * RANK), :] = ph
    rs_step(A2, 1)
    rs_finish(W1)
    wait_loads(reload)
    right_of(ph)
    reduce_right[0]()
    rs_step(A1, 0)
    rs_step(O1, 1)
    reduce_right[1]()
    rs_finish(O2)
    reduce_right[2]()
    rs_finish(A2)
    reduce_right[3]()
    rs_step(A1, 1)
    for step in reduce_right[4:]:
        step()
    rs_finish(O1)
    rs_finish(A1)
    outs[2].start()
    b.right_out[...] = right_out[pl.ds(0, slots * RANK), :] * 0.25
    b.small_out[...] = half_of(
        core, left_out[pl.ds(slots * RANK, 16), pl.ds(pl.multiple_of(z * 128, 128), 128)] * 0.25
    )

    close_right()
    for k in hops:
        small_along(k).wait_send()
    for g in range(6):
        for k in hops:
            ag_along(g, k).wait_send()
            for j in range(3):
                ag_beside(g, k, j).wait_send()
            rs_ring(g, k).wait_send()
        for k in range(chips):
            ag_core(g, k).wait_send()
        rs_pair(g).wait_send()
    for copy in outs:
        copy.wait()


def state_copies(parts, buffer, sem, first, outward=False):
    attn_i, attn_o, ffn_i, ffn_o = parts
    pairs = [(attn_i, buffer.at[pl.ds(0, 6)]), (attn_o, buffer.at[pl.ds(6, 2)])]
    columns = buffer.shape[2]
    for c in range(4):
        pairs.append((ffn_i.at[0, :, pl.ds(c * columns, columns)], buffer.at[8 + c]))
    pairs.append((ffn_o, buffer.at[pl.ds(12, 4)]))
    copies = []
    for n, (outer, inner) in enumerate(pairs):
        src, dst = (inner, outer) if outward else (outer, inner)
        copies.append(pltpu.make_async_copy(src, dst, sem.at[first + n]))
    return copies


def update_kernel(*refs):
    k = types.SimpleNamespace()
    (k.layer_in, k.grad_in, k.total, k.own, k.right, k.small_mean) = refs[:6]
    states_in, (k.small, k.small_mom, k.small_avg, k.layer_out, k.in_grad) = refs[6:22], refs[22:27]
    states_out, smalls_out = refs[27:43], refs[43:46]
    (k.fac_ai, k.fac_ao, k.fac_fi, k.fac_fo) = refs[46:50]
    (k.sums, k.weight, k.moment, k.error, k.average, k.via_low, k.via_full, k.in_sem, k.out_sem,
     k.pass_sem) = refs[50:]
    passing = [
        (pltpu.make_async_copy(src, via, k.pass_sem.at[n]), pltpu.make_async_copy(via, dst, k.pass_sem.at[3 + n]))
        for n, (src, via, dst) in enumerate(
            ((k.layer_in, k.via_low, k.layer_out), (k.grad_in, k.via_full, k.in_grad))
        )
    ]
    buffers = (k.weight, k.moment, k.error, k.average)
    sums = pltpu.make_async_copy(k.total, k.sums, k.pass_sem.at[2])
    sums.start()
    loads, stores = [
        [
            state_copies(states[4 * n : 4 * n + 4], buffer, sem, 7 * n, outward)
            for n, buffer in enumerate(buffers)
        ]
        for states, sem, outward in ((states_in, k.in_sem, False), (states_out, k.out_sem, True))
    ]
    order = [(0, range(0, 6)), (1, range(6, 8))] + [(2 + c, [8 + c]) for c in range(4)] + [(6, range(12, 16))]
    for n, _ in order:
        for state in loads:
            state[n].start()
    for copy, _ in passing:
        copy.start()
    right = k.right[...]
    k.fac_ai[...] = right[: 6 * RANK].reshape(6, RANK, -1)
    k.fac_ao[...] = right[6 * RANK : 8 * RANK].reshape(2, RANK, -1)
    width = right.shape[1]
    for c in range(4):
        k.fac_fi[0, :, pl.ds(c * width, width)] = right[(8 + c) * RANK : (9 + c) * RANK]
    k.fac_fo[0] = right[12 * RANK :]

    def step(weight, moment, average, update, rate):
        moment_new = MOMENTUM * moment + update
        weight_new = weight - rate * moment_new
        return weight_new, moment_new, average + AVERAGE * (weight_new - average)

    smalls_out[0][...], smalls_out[1][...], smalls_out[2][...] = step(
        k.small[...], k.small_mom[...], k.small_avg[...],
        k.small_mean[pl.ds(0, k.small.shape[0]), :], VECTOR_RATE,
    )
    sums.wait()
    for n, pieces in order:
        for state in loads:
            state[n].wait()
        for piece in pieces:
            slot, factor = (piece, piece) if piece < 8 else (8, piece) if piece < 12 else (piece - 3, 12)
            approx = dot_tn(
                k.own[pl.ds(slot * RANK, RANK), :], right[factor * RANK : (factor + 1) * RANK],
                FULL_PRECISION,
            )
            k.error[piece] = k.sums[piece] + k.error[piece] - approx
            k.weight[piece], k.moment[piece], k.average[piece] = step(
                k.weight[piece], k.moment[piece], k.average[piece], approx, LEARN_RATE
            )
        for state in stores:
            state[n].start()
    for incoming, outgoing in passing:
        incoming.wait()
        outgoing.start()
    for state in stores:
        for copy in state:
            copy.wait()
    for _, copy in passing:
        copy.wait()


def local_kernel(*refs):
    b = types.SimpleNamespace()
    (b.sid, b.rank, b.ham, b.dec, b.tgt, b.enc_in, b.og_in) = refs[:7]
    refs = refs[7:]
    b.weights, b.small, layer_out, in_grad_out, b.grads, b.small_grad = (
        refs[:6], refs[6], refs[7], refs[8], refs[9:15], refs[15],
    )
    for key, ref in zip(SCRATCH[:-1], refs[16:]):
        setattr(b, key, ref)
    sem = refs[-1]
    pairs = ((b.dec, b.x), (b.tgt, b.da), (b.enc_in, b.enc), (b.og_in, b.og))
    loads = [pltpu.make_async_copy(src, dst, sem.at[n]) for n, (src, dst) in enumerate(pairs)]
    outs = [pltpu.make_async_copy(b.og, layer_out, sem.at[4]), pltpu.make_async_copy(b.in_grad, in_grad_out, sem.at[5])]
    for copy in loads:
        copy.start()

    def hook(name):
        if name == "inputs":
            for copy in loads:
                copy.wait()
        if name in ("layer_out", "in_grad"):
            outs[name == "in_grad"].start()

    layer_math(b, hook)
    for copy in outs:
        copy.wait()


SCRATCH = list(math_scratch(1024, 512, 2048, 16))
VM = pl.BlockSpec(memory_space=pltpu.VMEM)
HBM = pl.BlockSpec(memory_space=pl.ANY)
SM = pl.BlockSpec(memory_space=pltpu.SMEM)


def padded(small):
    return jnp.pad(small, ((0, 16 - small.shape[0]), (0, 0)))


def run_local(sid, rank, ham, dec, tgt, enc, og, weights, small):
    (length, width), hidden = dec.shape, weights[W1].shape[-1]
    sds = jax.ShapeDtypeStruct
    scratch = math_scratch(length, width, hidden, 16)
    scratch.pop("small_grad")
    grads = [sds(w.shape[:2] + (w.shape[2] * w.shape[3], w.shape[4]), BF) for w in weights]
    return pl.pallas_call(
        local_kernel,
        out_shape=[sds(dec.shape, BF), sds(dec.shape, F32)] + grads + [sds((16, width), F32)],
        in_specs=[VM, VM, SM] + [HBM] * 4 + [VM] * 7,
        out_specs=[HBM, HBM] + [VM] * 7,
        scratch_shapes=list(scratch.values()) + [pltpu.SemaphoreType.DMA((6,))],
        compiler_params=pltpu.CompilerParams(vmem_limit_bytes=VMEM_BYTES),
        name="layer",
    )(sid, rank, ham, dec, tgt, enc, og, *weights, padded(small))


def run_step(chips, acts, weights_in, small_in, errors, factors):
    length, width = acts[3].shape
    hidden = weights_in[2].shape[2]
    sds = jax.ShapeDtypeStruct
    dma = pltpu.SemaphoreType.DMA
    columns = [3 * width, width, 3 * width, width, hidden, width]
    rows = [weights_in[0].shape[1]] * 5 + [weights_in[3].shape[1]]
    slots = 13
    weights = [pltpu.VMEM((chips, 2, 4, r // 4, c), BF) for r, c in zip(rows, columns)]
    grads = [pltpu.VMEM((chips, 2, r, c), BF) for r, c in zip(rows, columns)]
    pair_in = [pltpu.VMEM((chips, r, c), BF) for r, c in zip(rows, columns)]
    land = [pltpu.VMEM((chips - 1, r, c), BF) for r, c in zip(rows, columns)]
    sums = pltpu.VMEM((128, width), F32)
    return pl.pallas_call(
        lambda *refs: step_kernel(chips, *refs),
        out_shape=(
            sds((length, width), BF), sds((length, width), F32), sds((length, width), F32),
            sds((slots * RANK, 64), F32), sds((slots * RANK, width), F32), sds((16, 64), F32),
        ),
        in_specs=[VM, VM, SM] + [HBM] * 8 + [VM] + [HBM] * 4 + [VM] * 4,
        out_specs=(HBM, HBM, HBM, VM, VM, VM),
        scratch_shapes=list(math_scratch(length, width, hidden, 16).values())
        + weights + grads + pair_in + land
        + [
            pltpu.VMEM((16, width), F32), pltpu.VMEM((16, 128), BF), pltpu.VMEM((chips, 16, 128), BF),
            pltpu.VMEM((slots, 4 * RANK, width), BF), pltpu.VMEM((slots * RANK, 64), F32),
            sums, sums, sums, sums,
            pltpu.VMEM((2, 64 + 16 * (chips + 2), width), F32),
            dma((48,)),
            dma((6, chips - 1, 4)), dma((6, chips - 1, 4)), dma((6, chips)), dma((6, chips)),
            dma((6, chips)), dma((6, chips)), dma((2, chips + 7)), dma((2, chips + 7)),
            dma((chips,)), dma((chips,)), dma((3,)),
        ],
        compiler_params=pltpu.CompilerParams(
            vmem_limit_bytes=VMEM_BYTES, collective_id=0, has_side_effects=True
        ),
        name="step",
    )(*acts, *weights_in, small_in, *errors, *factors)


def run_update(layer_out, in_grad, total, own, right, small_mean, states, smalls):
    sds = jax.ShapeDtypeStruct
    like = [sds(s.shape, s.dtype) for group in states for s in group]
    dma = pltpu.SemaphoreType.DMA
    width = right.shape[1]
    state = pltpu.VMEM((16, 64, width), F32)
    faced = [sds(s, F32) for s in ((6, RANK, width), (2, RANK, width), (1, RANK, 4 * width), (1, RANK, width))]
    return pl.pallas_call(
        update_kernel,
        out_shape=[sds(layer_out.shape, layer_out.dtype), sds(in_grad.shape, in_grad.dtype)]
        + like + [sds(s.shape, F32) for s in smalls] + faced,
        in_specs=[HBM] * 3 + [VM] * 3 + [HBM] * 16 + [VM] * 3,
        out_specs=[HBM] * 18 + [VM] * 7,
        scratch_shapes=[state] * 5
        + [pltpu.VMEM(layer_out.shape, BF), pltpu.VMEM(in_grad.shape, F32)]
        + [dma((28,)), dma((28,)), dma((5,))],
        compiler_params=pltpu.CompilerParams(vmem_limit_bytes=VMEM_BYTES),
        name="update",
    )(layer_out, in_grad, total, own, right, small_mean, *[s for group in states for s in group], *smalls)


def fused_body(
    chips, decoder_input, target_embed, encoder_states, sentence_ids, position_ranks, hamming_counts,
    output_grad, attn_in, attn_out, ffn_in, ffn_out, small_params, attn_in_mom, attn_out_mom, ffn_in_mom,
    ffn_out_mom, small_mom, attn_in_err, attn_out_err, ffn_in_err, ffn_out_err, attn_in_fac, attn_out_fac,
    ffn_in_fac, ffn_out_fac, attn_in_avg, attn_out_avg, ffn_in_avg, ffn_out_avg, small_avg,
):
    masters = [attn_in, attn_out, ffn_in, ffn_out]
    errors = [attn_in_err[0], attn_out_err[0], ffn_in_err[0], ffn_out_err[0]]
    factors = [jnp.swapaxes(f, 1, 2) for f in (attn_in_fac, attn_out_fac, ffn_in_fac, ffn_out_fac)]
    acts = [
        sentence_ids, position_ranks, hamming_counts,
        decoder_input[0], target_embed[0], encoder_states[0], output_grad[0],
    ]
    layer_out, in_grad, total, own, right, small_mean = run_step(
        chips, acts, masters, small_params, errors, factors
    )
    width = right.shape[1]

    def pieces(group):
        return [group[0], group[1], group[2], group[3].reshape(4, 64, width)]

    states = [
        pieces(masters),
        pieces([attn_in_mom, attn_out_mom, ffn_in_mom, ffn_out_mom]),
        pieces(errors),
        pieces([attn_in_avg, attn_out_avg, ffn_in_avg, ffn_out_avg]),
    ]
    found = run_update(
        layer_out, in_grad, total.reshape(16, 64, width), own, right, small_mean, states,
        [small_params, small_mom, small_avg],
    )
    layer_out, in_grad, found = found[0], found[1], found[2:]
    new = [list(found[4 * n : 4 * n + 4]) for n in range(4)]
    for group in new:
        group[3] = group[3].reshape(ffn_out.shape)
    weights, moments, errs, averages = new
    small_new, small_mom_new, small_avg_new = found[16:19]
    fac = [jnp.swapaxes(f, 1, 2) for f in found[19:]]
    return (
        layer_out[None], in_grad[None], *weights, small_new, *moments, small_mom_new,
        *[e[None] for e in errs], *fac, *averages, small_avg_new,
    )


def body(
    decoder_input,
    target_embed,
    encoder_states,
    sentence_ids,
    position_ranks,
    hamming_counts,
    output_grad,
    attn_in,
    attn_out,
    ffn_in,
    ffn_out,
    small_params,
    attn_in_mom,
    attn_out_mom,
    ffn_in_mom,
    ffn_out_mom,
    small_mom,
    attn_in_err,
    attn_out_err,
    ffn_in_err,
    ffn_out_err,
    attn_in_fac,
    attn_out_fac,
    ffn_in_fac,
    ffn_out_fac,
    attn_in_avg,
    attn_out_avg,
    ffn_in_avg,
    ffn_out_avg,
    small_avg,
):
    small_full = lax.all_gather(
        small_params.astype(BF), "wide", axis=1, tiled=True
    ).astype(F32)

    def columns(stack):
        return jnp.swapaxes(stack, 0, 1).reshape(stack.shape[1], -1)

    def gather(rows):
        return lax.all_gather(rows.astype(BF), "wide", axis=0, tiled=True)

    whole = [
        gather(columns(attn_in[:3])), gather(attn_out[0]),
        gather(columns(attn_in[3:])), gather(attn_out[1]),
        gather(ffn_in[0]), gather(ffn_out[0]),
    ]
    length = decoder_input.shape[1]
    layer_out, input_grad, *grads, small_grad = run_local(
        sentence_ids, position_ranks, hamming_counts, decoder_input[0], target_embed[0],
        encoder_states[0], output_grad[0],
        [w.reshape(4, 2, 4, -1, w.shape[1]) for w in whole], small_full,
    )
    ga1, go1, ga2, go2, g1, g2 = [g.reshape(-1, g.shape[-1]) for g in grads]
    small_grad = small_grad[: small_full.shape[0]]

    def scatter(rows):
        return lax.psum_scatter(rows, "wide", scatter_dimension=0, tiled=True).astype(F32)

    def stack_of(rows):
        return jnp.swapaxes(rows.reshape(rows.shape[0], -1, g1.shape[0]), 0, 1)

    second, first = scatter(g2), scatter(g1)
    out_two, in_two, out_one, in_one = scatter(go2), scatter(ga2), scatter(go1), scatter(ga1)
    shards = (
        jnp.concatenate([stack_of(in_one), stack_of(in_two)], axis=0),
        jnp.stack([out_one, out_two]),
        first[None],
        second[None],
        lax.psum_scatter(small_grad, "wide", scatter_dimension=1, tiled=True),
    )
    scaling = (length * lax.axis_size("wide")) ** (-0.5)
    replicas = lax.axis_size("rep")
    fulls, lefts = ([], [])
    for gradient, error, factor_in in zip(
        shards[:4],
        (attn_in_err, attn_out_err, ffn_in_err, ffn_out_err),
        (attn_in_fac, attn_out_fac, ffn_in_fac, ffn_out_fac),
    ):
        full_grad = gradient * scaling + error[0]
        fulls.append(full_grad)
        lefts.append(jnp.einsum("knm,kmq->knq", full_grad, factor_in, precision=FULL_PRECISION))
    summed = lax.psum((lefts[0], lefts[1], lefts[2], lefts[3], shards[4] * scaling), "rep")
    left_mean = [piece / replicas for piece in summed[:4]]
    local_grams = [
        jnp.einsum("knq,kns->kqs", piece, piece, precision=FULL_PRECISION) for piece in left_mean
    ]
    grams = lax.psum((local_grams[0], local_grams[1], local_grams[2], local_grams[3]), "wide")
    orthos, rights = ([], [])
    for full_grad, piece, gram in zip(fulls, left_mean, grams):
        cholesky_factor = jnp.linalg.cholesky(gram)
        orthonormal = jnp.swapaxes(
            jax.scipy.linalg.solve_triangular(
                cholesky_factor, jnp.swapaxes(piece, 1, 2), lower=True
            ),
            1,
            2,
        )
        orthos.append(orthonormal)
        rights.append(jnp.einsum("knm,knq->kmq", full_grad, orthonormal, precision=FULL_PRECISION))
    right_sums = lax.psum((rights[0], rights[1], rights[2], rights[3]), ("rep", "wide"))
    reduced, new_errors, new_factors = ([], [], [])
    for full_grad, orthonormal, right_sum in zip(fulls, orthos, right_sums):
        right_mean = right_sum / replicas
        approx = jnp.einsum("knq,kmq->knm", orthonormal, right_mean, precision=FULL_PRECISION)
        reduced.append(approx)
        new_errors.append((full_grad - approx)[None])
        new_factors.append(right_mean)
    reduced.append(summed[4] / replicas)
    masters = (attn_in, attn_out, ffn_in, ffn_out, small_params)
    momenta = (attn_in_mom, attn_out_mom, ffn_in_mom, ffn_out_mom, small_mom)
    averages = (attn_in_avg, attn_out_avg, ffn_in_avg, ffn_out_avg, small_avg)
    rates = (LEARN_RATE, LEARN_RATE, LEARN_RATE, LEARN_RATE, VECTOR_RATE)
    new_weights, new_momenta, new_averages = ([], [], [])
    for master, moment, average, update, rate in zip(masters, momenta, averages, reduced, rates):
        moment_new = MOMENTUM * moment + update
        weight_new = master - rate * moment_new
        new_weights.append(weight_new)
        new_momenta.append(moment_new)
        new_averages.append(average + AVERAGE * (weight_new - average))
    return (
        layer_out[None],
        input_grad[None],
        new_weights[0],
        new_weights[1],
        new_weights[2],
        new_weights[3],
        new_weights[4],
        new_momenta[0],
        new_momenta[1],
        new_momenta[2],
        new_momenta[3],
        new_momenta[4],
        new_errors[0],
        new_errors[1],
        new_errors[2],
        new_errors[3],
        new_factors[0],
        new_factors[1],
        new_factors[2],
        new_factors[3],
        new_averages[0],
        new_averages[1],
        new_averages[2],
        new_averages[3],
        new_averages[4],
    )


def solution(mesh):
    placed = (
        P(("rep", "wide"), None, None),
        P(("rep", "wide"), None, None),
        P(("rep", "wide"), None, None),
        P(("rep", "wide"), None),
        P(("rep", "wide"), None),
        P(("rep", "wide"), None),
        P(("rep", "wide"), None, None),
        P(None, "wide", None),
        P(None, "wide", None),
        P(None, "wide", None),
        P(None, "wide", None),
        P(None, "wide"),
        P(None, "wide", None),
        P(None, "wide", None),
        P(None, "wide", None),
        P(None, "wide", None),
        P(None, "wide"),
        P("rep", None, "wide", None),
        P("rep", None, "wide", None),
        P("rep", None, "wide", None),
        P("rep", None, "wide", None),
        P(),
        P(),
        P(),
        P(),
        P(None, "wide", None),
        P(None, "wide", None),
        P(None, "wide", None),
        P(None, "wide", None),
        P(None, "wide"),
    )
    wide = mesh.shape["wide"]
    fused = mesh.shape["rep"] == 4 and wide == 8
    return jax.shard_map(
        functools.partial(fused_body, wide // 2) if fused else body,
        mesh=mesh,
        in_specs=placed,
        out_specs=(
            P(("rep", "wide"), None, None),
            P(("rep", "wide"), None, None),
            P(None, "wide", None),
            P(None, "wide", None),
            P(None, "wide", None),
            P(None, "wide", None),
            P(None, "wide"),
            P(None, "wide", None),
            P(None, "wide", None),
            P(None, "wide", None),
            P(None, "wide", None),
            P(None, "wide"),
            P("rep", None, "wide", None),
            P("rep", None, "wide", None),
            P("rep", None, "wide", None),
            P("rep", None, "wide", None),
            P(),
            P(),
            P(),
            P(),
            P(None, "wide", None),
            P(None, "wide", None),
            P(None, "wide", None),
            P(None, "wide", None),
            P(None, "wide"),
        ),
        check_vma=False,
    )
```

```python
import functools
import types

import jax
import jax.numpy as jnp
from jax import lax
from jax.experimental import pallas as pl
from jax.experimental.pallas import tpu as pltpu
from jax.sharding import PartitionSpec as P

HEADS = 8
HEAD_DIM = 64
RANK = 8
BLOCK = 256
SPAN = 128
TOGETHER = 2
EPS = 1e-05
FAR = -(2.0**30)
BF = jnp.bfloat16
F32 = jnp.float32
FULL_PRECISION = lax.Precision.HIGHEST
MOMENTUM = 0.9
LEARN_RATE = 0.1
VECTOR_RATE = 0.5
AVERAGE = 0.25
MESH = pl.DeviceIdType.MESH
VMEM_BYTES = 64 * 2**20 - 2**16

A1, O1, A2, O2, W1, W2 = range(6)


def dot(a, b, precision=None):
    return lax.dot_general(
        a, b, (((1,), (0,)), ((), ())), precision=precision, preferred_element_type=F32
    )


def dot_nt(a, b, precision=None):
    return lax.dot_general(
        a, b, (((1,), (1,)), ((), ())), precision=precision, preferred_element_type=F32
    )


def dot_tn(a, b, precision=None):
    return lax.dot_general(
        a, b, (((0,), (0,)), ((), ())), precision=precision, preferred_element_type=F32
    )


def gelu_pair(u):
    half = 0.5 * (1.0 + lax.erf(u * 0.7071067811865476))
    return u * half, half + u * jnp.exp(-0.5 * u * u) * 0.3989422804014327


def wide4(col):
    return jnp.concatenate([col] * 4, axis=1)


def norm_parts(resid):
    center = resid - jnp.mean(resid, axis=-1, keepdims=True)
    inv = lax.rsqrt(jnp.mean(center * center, axis=-1, keepdims=True) + EPS)
    return center * inv, inv


def norm_back(up, gain, normed, inv):
    scaled = up * gain
    return inv * (
        scaled
        - jnp.mean(scaled, axis=-1, keepdims=True)
        - normed * jnp.mean(scaled * normed, axis=-1, keepdims=True)
    )


def split_heads(pair):
    first = lax.broadcasted_iota(jnp.int32, pair.shape, 1) < HEAD_DIM
    zero = jnp.zeros_like(pair)
    return jnp.concatenate([jnp.where(first, pair, zero), jnp.where(first, zero, pair)], axis=0)


def join_heads(value):
    return jnp.concatenate(
        [value[:HEAD_DIM, :SPAN], value[HEAD_DIM:, SPAN:]], axis=0
    ).T


PAIRS = [pl.ds(128 * pair, 128) for pair in range(HEADS // 2)]


def spans(length):
    for i in range(length // SPAN):
        start, end = max(0, (i - 1) * SPAN), min(length, (i + 2) * SPAN)
        yield i, pl.ds(i * SPAN, SPAN), pl.ds(start, end - start)


def scores(b, q_both, k, rows, keys):
    near = b.near_q[rows, :]
    near = jnp.concatenate([near, near], axis=0)
    far = b.far_k[keys, :]
    return [
        dot_nt(jnp.concatenate([k[keys, p], far], axis=1), jnp.concatenate([both, near], axis=1))
        for p, both in zip(PAIRS, q_both)
    ]


def attend(b, q, k, v_t, o, lse, hook):
    for i, rows, keys in spans(q.shape[0]):
        s = scores(b, [split_heads(q[rows, p]) for p in PAIRS], k, rows, keys)
        peak = [jnp.max(one, axis=0, keepdims=True) for one in s]
        e = [jnp.exp(one - top) for one, top in zip(s, peak)]
        total = [jnp.sum(one, axis=0, keepdims=True) for one in e]
        prob = [(one * (1.0 / norm)).astype(BF) for one, norm in zip(e, total)]
        mixed = [dot(v_t[p, keys], one) for p, one in zip(PAIRS, prob)]
        for n, p in enumerate(PAIRS):
            lse[i * len(PAIRS) + n] = peak[n] + jnp.log(total[n])
            o[rows, p] = join_heads(mixed[n]).astype(BF)
        if i % 2:
            hook(i // 2)


def attend_back(b, q, k, v, k_t, do, lse, dqkv, sums, hook):
    length, width = q.shape
    last = length // SPAN - 1
    for i, rows, keys in spans(length):
        q_both = [split_heads(q[rows, p]) for p in PAIRS]
        d_both = [split_heads(do[rows, p]) for p in PAIRS]
        s = scores(b, q_both, k, rows, keys)
        dp = [dot_nt(v[keys, p], both) for p, both in zip(PAIRS, d_both)]
        prob = [jnp.exp(one - lse[i * len(PAIRS) + n]) for n, one in enumerate(s)]
        diag = [jnp.sum(x * y, axis=0, keepdims=True) for x, y in zip(prob, dp)]
        ds = [(x * (y - z)).astype(BF) for x, y, z in zip(prob, dp, diag)]
        low = [x.astype(BF) for x in prob]
        for n, p in enumerate(PAIRS):
            parts = (dot(ds[n], q_both[n]), dot(low[n], d_both[n]))
            for m, j in enumerate(range(max(0, i - 1), min(last, i + 1) + 1)):
                for which, part in enumerate(parts):
                    at = (pl.ds((3 * which + j % 3) * SPAN, SPAN), p)
                    piece = part[m * SPAN : (m + 1) * SPAN]
                    if i == max(0, j - 1):
                        sums[at] = piece
                    else:
                        sums[at] += piece
        dq_t = [dot(k_t[p, keys], one) for p, one in zip(PAIRS, ds)]
        for n, p in enumerate(PAIRS):
            dqkv[rows, p] = (join_heads(dq_t[n]) * HEAD_DIM ** (-0.5)).astype(BF)
        for j in [i - 1] * (i > 0) + [i] * (i == last):
            for which in range(2):
                done = sums[pl.ds((3 * which + j % 3) * SPAN, SPAN), :]
                dqkv[pl.ds(j * SPAN, SPAN), pl.ds((1 + which) * width, width)] = done.astype(BF)
        if i % 2:
            hook(i // 2)


def flat(ref, *at):
    value = ref[at] if at else ref[...]
    return value.reshape(-1, value.shape[-1])


def columns_of(ref, first, count):
    return flat(ref, *(slice(None),) * (len(ref.shape) - 1), pl.ds(first, count))


def layer_math(b, hook):
    w, g = b.weights, b.grads
    length, width = b.x.shape
    blocks = length // BLOCK
    chips = w[A1].shape[0]
    hidden = w[W1].shape[-1]
    parts = hidden // 512
    scale = jnp.asarray(HEAD_DIM ** (-0.5), BF)
    row = lambda r: b.small[pl.ds(r, 1), :]

    def each_block(body):
        for i in range(blocks):
            body(pl.ds(i * BLOCK, BLOCK))

    sent = b.sid[...]
    per_pos = jnp.zeros_like(sent)
    for s in range(b.ham.shape[1]):
        per_pos = jnp.where(sent == s, b.ham[0, s], per_pos)
    glance = jnp.where(2 * b.rank[...] < per_pos, 1.0, 0.0).astype(F32)
    sent_f = sent.astype(F32)
    b.col[...] = jnp.broadcast_to(glance, (128, length)).T
    hook("inputs")

    @each_block
    def _(rows):
        b.x[rows, :] = jnp.where(
            wide4(b.col[rows, :]) > 0.5, b.da[rows, :].astype(F32), b.x[rows, :].astype(F32)
        ).astype(BF)

    hook("mixed")
    b.col[...] = jnp.broadcast_to(sent_f, (128, length)).T

    @each_block
    def _(rows):
        here = b.col[rows, :]
        same = lax.broadcasted_iota(jnp.int32, here.shape, 1).astype(F32) == here
        b.near_q[rows, :] = jnp.where(same, 1.0, 0.0).astype(BF)
        b.far_k[rows, :] = jnp.where(same, 0.0, FAR).astype(BF)

    hook("masked")

    @each_block
    def _(rows):
        x_blk = b.x[rows, :]
        b.q1[rows, :] = dot(x_blk, columns_of(w[A1], 0, width)).astype(BF) * scale
        b.k1[rows, :] = dot(x_blk, columns_of(w[A1], width, width)).astype(BF)
        v = dot(x_blk, columns_of(w[A1], 2 * width, width)).astype(BF)
        b.v1[rows, :] = v
        b.turn[:, rows] = v.T

    hook("qkv1")
    attend(b, b.q1, b.k1, b.turn, b.o1, b.lse1, lambda i: hook(("attend1", i)))
    hook("need_small")
    hook(("need", O1))
    hook(("need", A2))

    @each_block
    def _(rows):
        resid = b.x[rows, :].astype(F32) + dot(b.o1[rows, :], flat(w[O1]))
        normed, inv = norm_parts(resid)
        b.n1[rows, :] = normed
        b.col[rows, :] = jnp.broadcast_to(inv, (BLOCK, 128))
        h1b = (normed * row(0) + row(1)).astype(BF)
        b.q2[rows, :] = dot(h1b, columns_of(w[A2], 0, width)).astype(BF) * scale
        e_blk = b.enc[rows, :]
        b.k2[rows, :] = dot(e_blk, columns_of(w[A2], width, width)).astype(BF)
        v = dot(e_blk, columns_of(w[A2], 2 * width, width)).astype(BF)
        b.v2[rows, :] = v
        b.turn[:, rows] = v.T

    hook("qkv2")
    attend(b, b.q2, b.k2, b.turn, b.o2, b.lse2, lambda i: hook(("attend2", i)))
    hook(("need", O2))
    hook(("need", W1))

    b.small_grad[...] = jnp.zeros_like(b.small_grad)

    def add_small(r, value):
        b.small_grad[pl.ds(r, 1), :] += jnp.sum(value, axis=0, keepdims=True)

    per = hidden // chips
    chunk = [pl.ds(c * 512, 512) for c in range(parts)]
    for first in range(0, blocks, TOGETHER):
        group = [pl.ds((first + n) * BLOCK, BLOCK) for n in range(TOGETHER)]
        h1 = [b.n1[rows, :] * row(0) + row(1) for rows in group]
        resid = [h + dot(b.o2[rows, :], flat(w[O2])) for h, rows in zip(h1, group)]
        normed2, inv2 = zip(*[norm_parts(r) for r in resid])
        h2 = [n * row(2) + row(3) for n in normed2]
        h2_low = [h.astype(BF) for h in h2]
        for n, rows in enumerate(group):
            b.n2[pl.ds(n * BLOCK, BLOCK), :] = normed2[n]
            b.inv2[pl.ds(n * BLOCK, BLOCK), :] = jnp.broadcast_to(inv2[n], (BLOCK, 128))
            b.h2b[rows, :] = h2_low[n]
        for c in range(parts):
            us = [dot(h, columns_of(w[W1], c * 512, 512)) + row(7 + c) for h in h2_low]
            for n, rows in enumerate(group):
                act, der = gelu_pair(us[n])
                b.hid[rows, chunk[c]] = act.astype(BF)
                b.slope[pl.ds((n * parts + c) * BLOCK, BLOCK), :] = der
        if first == 0:
            hook("gelu")
            hook(("need", W2))
        resid3 = [
            h + (dot(b.hid[rows, :], flat(w[W2])) + row(6)) for h, rows in zip(h2, group)
        ]
        normed3, inv3 = zip(*[norm_parts(r) for r in resid3])
        ups = [b.og[rows, :].astype(F32) for rows in group]
        dr3 = [norm_back(up, row(4), n, i) for up, n, i in zip(ups, normed3, inv3)]
        dz_low = [d.astype(BF) for d in dr3]
        for n, rows in enumerate(group):
            b.og[rows, :] = (normed3[n] * row(4) + row(5)).astype(BF)
            add_small(4, ups[n] * normed3[n])
            add_small(5, ups[n])
            b.dz[rows, :] = dz_low[n]
            add_small(6, dz_low[n].astype(F32))
        for c in range(chips):
            ds = [dot_nt(d, flat(w[W2], c)) for d in dz_low]
            for half in range(per // 512):
                at = c * (per // 512) + half
                for n, rows in enumerate(group):
                    part = ds[n][:, half * 512 : (half + 1) * 512]
                    low = (part * b.slope[pl.ds((n * parts + at) * BLOCK, BLOCK), :]).astype(BF)
                    b.du[rows, chunk[at]] = low
                    add_small(7 + at, low.astype(F32))
        dh2 = [d + dot_nt(b.du[rows, :], flat(w[W1])) for d, rows in zip(dr3, group)]
        normed2 = [b.n2[pl.ds(n * BLOCK, BLOCK), :] for n in range(TOGETHER)]
        inv2 = [b.inv2[pl.ds(n * BLOCK, BLOCK), :] for n in range(TOGETHER)]
        dr2 = [norm_back(d, row(2), n, wide4(i)) for d, n, i in zip(dh2, normed2, inv2)]
        da_low = [d.astype(BF) for d in dr2]
        do = [dot_nt(d, flat(w[O2])).astype(BF) for d in da_low]
        for n, rows in enumerate(group):
            add_small(2, dh2[n] * normed2[n])
            add_small(3, dh2[n])
            b.in_grad[rows, :] = dr2[n]
            b.da[rows, :] = da_low[n]
            b.do[rows, :] = do[n]

    hook("layer_out")

    for c in range(2 * chips):
        rows = hidden // (2 * chips)
        cols = pl.ds(c * rows, rows)
        g[W2][c // 2, c % 2] = dot_tn(b.hid[:, cols], b.dz[...]).astype(BF)

    hook(("grad", W2))

    def each_chip(body):
        per = width // chips
        for c in range(chips):
            body(c, pl.ds(c * per, per))

    def put(ref, c, first, value):
        shape = (2, value.shape[0] // 2, value.shape[1])
        ref[c, :, :, pl.ds(first, value.shape[1])] = value.astype(BF).reshape(shape)

    @each_chip
    def _(c, cols):
        put(g[W1], c, 0, dot_tn(b.h2b[:, cols], b.du[...]))

    hook(("grad", W1))

    @each_chip
    def _(c, cols):
        put(g[O2], c, 0, dot_tn(b.o2[:, cols], b.da[...]))

    hook(("grad", O2))

    dqkv = b.hid
    q_part, kv_part, all_part = pl.ds(0, width), pl.ds(width, 2 * width), pl.ds(0, 3 * width)

    def turn_keys(keys):
        @each_block
        def _(rows):
            b.turn[:, rows] = keys[rows, :].T

    turn_keys(b.k2)
    attend_back(
        b, b.q2, b.k2, b.v2, b.turn, b.do, b.lse2, dqkv, b.slope, lambda i: hook(("back2", i))
    )

    @each_block
    def _(rows):
        normed = b.n1[rows, :]
        b.h2b[rows, :] = (normed * row(0) + row(1)).astype(BF)
        dh1 = b.in_grad[rows, :] + dot_nt(dqkv[rows, q_part], columns_of(w[A2], 0, width))
        add_small(0, dh1 * normed)
        add_small(1, dh1)
        dr1 = norm_back(dh1, row(0), normed, wide4(b.col[rows, :]))
        b.in_grad[rows, :] = dr1
        da_low = dr1.astype(BF)
        b.da[rows, :] = da_low
        b.do[rows, :] = dot_nt(da_low, flat(w[O1])).astype(BF)

    hook("norm1")

    @each_chip
    def _(c, cols):
        put(g[A2], c, 0, dot_tn(b.h2b[:, cols], dqkv[:, q_part]))
        put(g[A2], c, width, dot_tn(b.enc[:, cols], dqkv[:, kv_part]))

    hook(("grad", A2))

    @each_chip
    def _(c, cols):
        put(g[O1], c, 0, dot_tn(b.o1[:, cols], b.da[...]))

    hook(("grad", O1))
    turn_keys(b.k1)
    attend_back(
        b, b.q1, b.k1, b.v1, b.turn, b.do, b.lse1, dqkv, b.slope, lambda i: hook(("back1", i))
    )

    @each_chip
    def _(c, cols):
        put(g[A1], c, 0, dot_tn(b.x[:, cols], dqkv[:, all_part]))

    hook(("grad", A1))

    @each_block
    def _(rows):
        b.in_grad[rows, :] += dot_nt(dqkv[rows, all_part], flat(w[A1]))

    hook("in_grad")


def math_scratch(length, width, hidden, small_rows):
    low, full = pltpu.VMEM((length, width), BF), pltpu.VMEM((length, width), F32)
    totals = pltpu.VMEM((length // SPAN * len(PAIRS), 1, 2 * SPAN), F32)
    marks = pltpu.VMEM((length, 128), BF)
    return dict(
        x=low, enc=low, og=low, q1=low, k1=low, v1=low, o1=low, q2=low, k2=low, v2=low, o2=low,
        turn=pltpu.VMEM((width, length), BF),
        n1=full, n2=pltpu.VMEM((TOGETHER * BLOCK, width), F32),
        inv2=pltpu.VMEM((TOGETHER * BLOCK, 128), F32),
        hid=pltpu.VMEM((length, hidden), BF), du=pltpu.VMEM((length, hidden), BF),
        dz=low, h2b=low, slope=pltpu.VMEM((TOGETHER * length, width), F32), in_grad=full, da=low, do=low,
        lse1=totals, lse2=totals, near_q=marks, far_k=marks,
        col=pltpu.VMEM((length, 128), F32),
        small_grad=pltpu.VMEM((small_rows, width), F32),
    )


def half_of(core, pair):
    return jnp.where(core == 0, pair[:, :64], pair[:, 64:])


def placed(core, part):
    zero = jnp.zeros_like(part)
    return jnp.where(
        core == 0, jnp.concatenate([part, zero], axis=1), jnp.concatenate([zero, part], axis=1)
    )


def split3(value):
    high = value.astype(BF).astype(F32)
    middle = (value - high).astype(BF).astype(F32)
    low = (value - high) - middle
    return jnp.concatenate([high, middle, low, jnp.zeros_like(value)], axis=0).astype(BF)


def add3(value):
    return value[:RANK] + value[RANK : 2 * RANK] + value[2 * RANK : 3 * RANK]


def orthonormal(rows_of, count):
    single = rows_of[: count * RANK].reshape(count, RANK, -1)
    rest = rows_of[count * RANK :].reshape(-1, RANK, rows_of.shape[1])
    joined = jnp.concatenate([rest[i] for i in range(rest.shape[0])], axis=1)[None]
    done = []
    for value in (single, joined):
        index = lax.broadcasted_iota(jnp.int32, value.shape, 1)
        for j in range(RANK):
            pivot = value[:, j : j + 1, :]
            unit = pivot / jnp.sqrt(jnp.sum(pivot * pivot, axis=-1, keepdims=True))
            along = jnp.sum(value * unit, axis=-1, keepdims=True)
            value = jnp.where(index < j, value, jnp.where(index == j, unit, value - along * unit))
        done.append(value)
    width = rows_of.shape[1]
    tail = [done[1][0, :, i * width : (i + 1) * width] for i in range(rest.shape[0])]
    return jnp.concatenate([done[0].reshape(count * RANK, width)] + tail, axis=0)


def step_kernel(chips, *refs):
    b = types.SimpleNamespace()
    (b.sid, b.rank, b.ham, b.dec, b.tgt, b.enc_in, b.og_in, b.attn_in, b.attn_out, b.ffn_in, b.ffn_out,
     b.small_in, b.err_ai, b.err_ao, b.err_fi, b.err_fo, b.fac_ai, b.fac_ao, b.fac_fi, b.fac_fo,
     b.layer_out, b.in_grad_out, b.total_out, b.own_out, b.right_out, b.small_out) = refs[:26]
    refs = refs[26:]
    for key, ref in zip(SCRATCH, refs):
        setattr(b, key, ref)
    refs = refs[len(SCRATCH) :]
    weights, grads, pair_in, land = (refs[n : n + 6] for n in (0, 6, 12, 18))
    (small, small_tile, small_land, fac3, err_left, left, left_out,
     right, right_out, inbox, load_sem, ag_send, ag_recv, cc_send, cc_recv, rs_send, rs_recv,
     ar_send, ar_recv, sm_send, sm_recv, out_sem) = refs[24:]
    b.weights, b.grads, b.small = weights, grads, small
    rep, wide = lax.axis_index("rep"), lax.axis_index("wide")
    core, z = wide % 2, wide // 2
    width = b.x.shape[1]
    slots = fac3.shape[0]
    singles = 9
    sibling = (rep, wide + 1 - 2 * core)
    beside = [(rep + 1 - 2 * (rep % 2), wide), ((rep + 2) % 4, wide), (3 - rep, wide)]
    ahead = [(z + k) % chips for k in range(1, chips)]
    behind = [(z + chips - k) % chips for k in range(1, chips)]
    along = [(rep, there * 2 + core) for there in ahead]

    def remote(src, dst, send, recv, to):
        return pltpu.make_async_remote_copy(
            src_ref=src, dst_ref=dst, send_sem=send, recv_sem=recv, device_id=to, device_id_type=MESH
        )

    master, error = b.in_grad, b.slope
    loads = []

    def load(src, dst):
        copy = pltpu.make_async_copy(src, dst, load_sem.at[len(loads)])
        copy.start()
        loads.append(copy)
        return copy

    def load_state(attn_i, attn_o, ffn_i, ffn_o, to):
        rows, found = [], []
        for s in range(6):
            found.append(load(attn_i.at[s], to.at[pl.ds(64 * s, 64)]))
        for s in range(2):
            found.append(load(attn_o.at[s], to.at[pl.ds(384 + 64 * s, 64)]))
        for c in range(4):
            found.append(
                load(ffn_i.at[0, :, pl.ds(c * width, width)], to.at[pl.ds(512 + 64 * c, 64)])
            )
        found.append(load(ffn_o.at[0], to.at[pl.ds(768, 256)]))
        return found

    masters = load_state(b.attn_in, b.attn_out, b.ffn_in, b.ffn_out, master)
    acts = [load(b.dec, b.x), load(b.tgt, b.da), load(b.enc_in, b.enc), load(b.og_in, b.og)]
    errors = load_state(b.err_ai, b.err_ao, b.err_fi, b.err_fo, error)

    barrier = pltpu.get_barrier_semaphore()
    partners = [sibling] + beside + along
    for partner in partners:
        pl.semaphore_signal(barrier, inc=1, device_id=partner, device_id_type=MESH)

    def ag_along(g, k):
        ref = weights[g].at[z, core, rep]
        return remote(ref, ref, ag_send.at[g, k, 0], ag_recv.at[g, k, 0], along[k])

    def ag_along_in(g, k):
        ref = weights[g].at[behind[k], core, rep]
        return remote(ref, ref, ag_send.at[g, k, 0], ag_recv.at[g, k, 0], along[k])

    def ag_beside(g, k, j):
        ref = weights[g].at[behind[k], core, rep]
        return remote(ref, ref, ag_send.at[g, k, 1 + j], ag_recv.at[g, k, 1 + j], beside[j])

    def ag_beside_in(g, k, j):
        ref = weights[g].at[behind[k], core, beside[j][0]]
        return remote(ref, ref, ag_send.at[g, k, 1 + j], ag_recv.at[g, k, 1 + j], beside[j])

    def ag_core(g, k):
        ref = weights[g].at[z if k == 0 else behind[k - 1], core]
        return remote(ref, ref, cc_send.at[g, k], cc_recv.at[g, k], sibling)

    def ag_core_in(g, k):
        ref = weights[g].at[z if k == 0 else behind[k - 1], 1 - core]
        return remote(ref, ref, cc_send.at[g, k], cc_recv.at[g, k], sibling)

    hops = range(chips - 1)

    def own_shard(g):
        quarter = weights[g].shape[3]

        def put(at, first, count):
            value = master[pl.ds(at, 4 * quarter), :].astype(BF)
            weights[g][z, core, :, :, pl.ds(first, count)] = value.reshape(4, quarter, count)

        if g in (A1, A2):
            for s in range(3):
                put(64 * (s + (3 if g == A2 else 0)), s * width, width)
        elif g in (O1, O2):
            put(384 + (64 if g == O2 else 0), 0, width)
        elif g == W1:
            for c in range(4):
                put(512 + 64 * c, c * width, width)
        else:
            put(768, 0, width)

    def ag_start(g):
        for k in hops:
            ag_along(g, k).start()
        ag_core(g, 0).start()

    def ag_forward(g):
        for k in hops:
            ag_along_in(g, k).wait_recv()
            for j in range(3):
                ag_beside(g, k, j).start()

    def ag_cross(g):
        for k in hops:
            for j in range(3):
                ag_beside_in(g, k, j).wait_recv()
            ag_core(g, k + 1).start()

    def ag_ready(g):
        for k in range(chips):
            ag_core_in(g, k).wait_recv()

    def small_along(k):
        return remote(small_tile, small_land.at[k], sm_send.at[k], sm_recv.at[k], along[k])

    small_core = remote(small_tile, small_land.at[chips - 1], sm_send.at[chips - 1], sm_recv.at[chips - 1], sibling)

    def small_start():
        rows = small_tile.shape[0] - b.small_in.shape[0]
        value = jnp.concatenate([b.small_in[...], jnp.zeros((rows, 64), F32)], axis=0)
        small_tile[...] = placed(core, value).astype(BF)
        small_core.start()

    def small_forward():
        small_core.wait_recv()
        small_core.wait_send()
        both = small_tile[...].astype(F32) + small_land[chips - 1].astype(F32)
        small_tile[...] = both.astype(BF)
        small[:, pl.ds(pl.multiple_of(z * 128, 128), 128)] = both
        for k in hops:
            small_along(k).start()

    def small_ready():
        for k in hops:
            small_along(k).wait_recv()
            small[:, pl.ds(pl.multiple_of(behind[k] * 128, 128), 128)] = small_land[k].astype(F32)

    def rs_pair(g):
        return remote(
            grads[g].at[:, 1 - core], pair_in[g], rs_send.at[g, 0], rs_recv.at[g, 0], sibling
        )

    def rs_ring(g, s):
        chunk = (z + chips - 1 - s) % chips
        return remote(
            pair_in[g].at[chunk], land[g].at[s], rs_send.at[g, 1 + s], rs_recv.at[g, 1 + s], along[0]
        )

    held = (A1, A2)

    def rs_start(g):
        rs_pair(g).start()

    def rs_add(g):
        rs_pair(g).wait_recv()
        for s in range(chips):
            chunk = (z + chips - 1 - s) % chips
            total = pair_in[g][chunk].astype(F32) + grads[g][chunk, core].astype(F32)
            pair_in[g][chunk] = total.astype(BF)
            if s == 0 and g not in held:
                rs_go(g)

    def rs_go(g):
        rs_ring(g, 0).start()

    def rs_step(g, s):
        rs_ring(g, s).wait_recv()
        chunk = (z + 2 * chips - 2 - s) % chips
        total = land[g][s].astype(F32) + pair_in[g][chunk].astype(F32)
        pair_in[g][chunk] = total.astype(BF)
        rs_ring(g, s + 1).start()

    total = b.n1

    def rs_finish(g):
        rs_ring(g, chips - 2).wait_recv()
        value = (land[g][chips - 2].astype(F32) + pair_in[g][z].astype(F32)) * scaling
        if g in (A1, A2):
            for s in range(3):
                total[pl.ds(64 * (s + (3 if g == A2 else 0)), 64), :] = value[:, s * width : (s + 1) * width]
        elif g in (O1, O2):
            total[pl.ds(384 + (64 if g == O2 else 0), 64), :] = value
        elif g == W1:
            for c in range(4):
                total[pl.ds(512 + 64 * c, 64), :] = value[:, c * width : (c + 1) * width]
        else:
            total[pl.ds(768, 256), :] = value

    length = b.x.shape[0]
    scaling = (length * 2 * chips) ** (-0.5)

    def all_reduce(which, source, result, inbox):
        rows = lambda start, count: pl.ds(pl.multiple_of(start, 16), count)
        half = lambda c: rows(c * 64, 64)
        part = lambda r: rows(core * 64 + r * 16, 16)
        mine = part(rep)
        move = lambda src, dst, n, to: remote(src, dst, ar_send.at[which, n], ar_recv.at[which, n], to)
        fold = move(source.at[half(1 - core)], inbox.at[pl.ds(0, 64)], 0, sibling)
        over = [
            move(source.at[part(beside[j][0])], inbox.at[pl.ds(64 + 16 * j, 16)], 1 + j, beside[j])
            for j in range(3)
        ]
        up = [
            move(source.at[mine], inbox.at[pl.ds(112 + 16 * k, 16)], 4 + k, along[k]) for k in hops
        ]
        first = 3 + chips
        back = [move(result.at[mine], result.at[mine], first + j, beside[j]) for j in range(3)]
        back_in = [
            move(result.at[part(beside[j][0])], result.at[part(beside[j][0])], first + j, beside[j])
            for j in range(3)
        ]
        share = move(result.at[half(core)], result.at[half(core)], first + 3, sibling)
        share_in = move(result.at[half(1 - core)], result.at[half(1 - core)], first + 3, sibling)

        def folded():
            fold.wait_recv()
            source[half(core), :] += inbox[pl.ds(0, 64), :]
            for copy in over:
                copy.start()

        def summed():
            for copy in over:
                copy.wait_recv()
            source[mine, :] += (inbox[pl.ds(64, 16), :] + inbox[pl.ds(80, 16), :]) + inbox[pl.ds(96, 16), :]
            for copy in up:
                copy.start()

        def whole():
            for copy in up:
                copy.wait_recv()
            value = None
            for there in range(chips):
                term = source[mine, :]
                for k in hops:
                    term = jnp.where(behind[k] == there, inbox[pl.ds(112 + 16 * k, 16), :], term)
                value = term if value is None else value + term
            result[mine, :] = value
            for copy in back:
                copy.start()

        def shared():
            for copy in back_in:
                copy.wait_recv()
            share.start()

        def finish():
            for copy in [fold, share] + over + up + back:
                copy.wait_send()

        return [fold.start, folded, summed, whole, shared, share_in.wait_recv], finish

    def error_left():
        for copy in errors:
            copy.wait()
        factor = lambda s: b.fac_ai[s] if s < 6 else b.fac_ao[s - 6] if s < 8 else (
            b.fac_fi[0, :, (s - 8) * width : (s - 7) * width] if s < 12 else b.fac_fo[0]
        )
        for s in range(slots):
            fac3[s] = split3(factor(s))
        piece = lambda at: error[pl.ds(at, 64), :]
        for s in range(slots):
            if s < 8:
                value = dot_nt(factor(s), piece(64 * s), FULL_PRECISION)
            elif s == 8:
                value = sum(dot_nt(factor(8 + c), piece(512 + 64 * c), FULL_PRECISION) for c in range(4))
            else:
                value = dot_nt(factor(12), piece(768 + 64 * (s - 9)), FULL_PRECISION)
            err_left[pl.ds(s * RANK, RANK), :] = value

    def grad_of(s):
        if s < 6:
            return [(columns_of(grads[A1 if s < 3 else A2], (s % 3) * width, width), s)]
        if s < 8:
            return [(flat(grads[O1 if s == 6 else O2]), s)]
        if s == 8:
            return [(columns_of(grads[W1], c * width, width), 8 + c) for c in range(4)]
        j = s - 9
        return [(flat(grads[W2], slice(None), slice(None), pl.ds(64 * j, 64)), 12)]

    def left_of(which):
        for s in which:
            value = None
            for matrix, f in grad_of(s):
                one = dot_nt(fac3[f], matrix)
                value = one if value is None else value + one
            left[pl.ds(s * RANK, RANK), :] = add3(value) * scaling

    def left_close():
        lanes = pl.ds(pl.multiple_of(z * 128, 128), 128)
        left[pl.ds(0, slots * RANK), lanes] += placed(core, err_left[...])
        left[pl.ds(slots * RANK, 16), :] = b.small_grad[...] * scaling
        left[pl.ds(slots * RANK + 16, 8), :] = jnp.zeros((8, width), F32)

    def right_of(ph):
        own = half_of(core, left[pl.ds(0, slots * RANK), pl.ds(pl.multiple_of(z * 128, 128), 128)])
        b.own_out[...] = own
        terms = [split3(ph[s * RANK : (s + 1) * RANK]) for s in range(slots)]
        piece = lambda at: error[pl.ds(at, 64), :]
        own_of = lambda s: own[s * RANK : (s + 1) * RANK]
        values = [None] * slots
        for s in range(slots):
            for matrix, f in grad_of(s):
                one = dot(terms[s], matrix)
                values[f] = one if values[f] is None else values[f] + one
        for f in range(slots):
            value = add3(values[f]) * scaling
            if f < 8:
                value += dot(own_of(f), piece(64 * f), FULL_PRECISION)
            elif f < 12:
                value += dot(own_of(8), piece(512 + 64 * (f - 8)), FULL_PRECISION)
            else:
                for j in range(4):
                    value += dot(own_of(9 + j), piece(768 + 64 * j), FULL_PRECISION)
            right[pl.ds(f * RANK, RANK), :] = value
        right[pl.ds(slots * RANK, 24), :] = jnp.zeros((24, width), F32)

    def prepare(g, needed):
        for n in needed:
            masters[n].wait()
        own_shard(g)

    prepare(A1, (0, 1, 2))
    pl.semaphore_wait(barrier, len(partners))
    ag_start(A1)
    prepare(O1, (6,))
    ag_start(O1)
    small_start()
    reduce_left, close_left = all_reduce(0, left, left_out, inbox.at[0])
    reduce_right, close_right = all_reduce(1, right, right_out, inbox.at[1])

    def wait_loads(which):
        for copy in which:
            copy.wait()

    reload = []

    def reload_errors():
        reload.extend(load_state(b.err_ai, b.err_ao, b.err_fi, b.err_fo, error))

    def out_copy(src, dst, i):
        return pltpu.make_async_copy(src, dst, out_sem.at[i])

    outs = [out_copy(b.og, b.layer_out, 0), out_copy(b.in_grad, b.in_grad_out, 1), out_copy(total, b.total_out, 2)]
    plan = {
        "inputs": [lambda: wait_loads(acts[:2])],
        "mixed": [
            lambda: prepare(A2, (3, 4, 5)), lambda: prepare(O2, (7,)), lambda: ag_forward(A1),
            lambda: ag_start(A2),
        ],
        "masked": [
            small_forward, lambda: ag_forward(O1), lambda: ag_start(O2),
            lambda: prepare(W1, (8, 9, 10, 11)), lambda: prepare(W2, (12,)), lambda: ag_start(W1),
            lambda: ag_cross(A1), error_left, lambda: ag_forward(A2), lambda: ag_start(W2),
            lambda: ag_ready(A1),
        ],
        "qkv1": [lambda: ag_cross(O1), lambda: ag_forward(O2)],
        ("attend1", 1): [lambda: ag_forward(W1)],
        ("attend1", 3): [lambda: ag_cross(A2)],
        "need_small": [small_ready, lambda: wait_loads(acts[2:])],
        "qkv2": [lambda: ag_cross(O2), lambda: ag_forward(W2)],
        ("attend2", 3): [lambda: ag_cross(W1)],
        "gelu": [lambda: ag_cross(W2)],
        "layer_out": [outs[0].start],
        ("grad", W2): [lambda: rs_start(W2)],
        ("grad", W1): [lambda: rs_add(W2), lambda: rs_start(W1)],
        ("grad", O2): [lambda: rs_start(O2)],
        ("back2", 0): [lambda: rs_add(W1), lambda: rs_add(O2)],
        "norm1": [lambda: rs_step(W2, 0)],
        ("grad", A2): [lambda: rs_start(A2)],
        ("grad", O1): [
            lambda: rs_start(O1), lambda: left_of((8, 9, 10, 11, 12, 7)),
        ],
        ("back1", 0): [lambda: rs_add(A2), lambda: rs_step(W1, 0)],
        ("back1", 1): [lambda: rs_add(O1), lambda: left_of((3, 4, 5, 6))],
        ("back1", 2): [lambda: rs_step(O2, 0)],
        ("back1", 3): [lambda: rs_step(W2, 1)],
        ("grad", A1): [
            lambda: rs_start(A1), lambda: left_of((0, 1, 2)), left_close, reduce_left[0],
            reload_errors, reduce_left[1],
        ],
        "in_grad": [outs[1].start],
    }
    for g in (O1, A2, O2, W1, W2):
        plan[("need", g)] = [lambda g=g: ag_ready(g)]

    def hook(name):
        for action in plan.pop(name, ()):
            action()

    layer_math(b, hook)

    reduce_left[2]()
    rs_go(A2)
    rs_step(W1, 1)
    rs_add(A1)
    rs_go(A1)
    rs_step(O2, 1)
    rs_step(O1, 0)
    for step in reduce_left[3:]:
        step()
    close_left()
    rs_step(A2, 0)
    ph = orthonormal(left_out[pl.ds(0, slots * RANK), :], singles)
    left[pl.ds(0, slots * RANK), :] = ph
    rs_finish(W2)
    rs_step(A1, 0)
    wait_loads(reload)
    right_of(ph)
    rs_step(A2, 1)
    reduce_right[0]()
    rs_finish(W1)
    reduce_right[1]()
    reduce_right[2]()
    rs_step(O1, 1)
    rs_step(A1, 1)
    rs_finish(O2)
    for step in reduce_right[3:]:
        step()
    rs_finish(A2)
    rs_finish(O1)
    rs_finish(A1)
    outs[2].start()
    b.right_out[...] = right_out[pl.ds(0, slots * RANK), :] * 0.25
    b.small_out[...] = half_of(
        core, left_out[pl.ds(slots * RANK, 16), pl.ds(pl.multiple_of(z * 128, 128), 128)] * 0.25
    )

    close_right()
    for k in hops:
        small_along(k).wait_send()
    for g in range(6):
        for k in hops:
            ag_along(g, k).wait_send()
            for j in range(3):
                ag_beside(g, k, j).wait_send()
            rs_ring(g, k).wait_send()
        for k in range(chips):
            ag_core(g, k).wait_send()
        rs_pair(g).wait_send()
    for copy in outs:
        copy.wait()


def state_copies(parts, buffer, sem, first, outward=False):
    attn_i, attn_o, ffn_i, ffn_o = parts
    pairs = [(attn_i, buffer.at[pl.ds(0, 6)]), (attn_o, buffer.at[pl.ds(6, 2)])]
    columns = buffer.shape[2]
    for c in range(4):
        pairs.append((ffn_i.at[0, :, pl.ds(c * columns, columns)], buffer.at[8 + c]))
    pairs.append((ffn_o, buffer.at[pl.ds(12, 4)]))
    copies = []
    for n, (outer, inner) in enumerate(pairs):
        src, dst = (inner, outer) if outward else (outer, inner)
        copies.append(pltpu.make_async_copy(src, dst, sem.at[first + n]))
    return copies


def update_kernel(*refs):
    k = types.SimpleNamespace()
    (k.layer_in, k.grad_in, k.total, k.own, k.right, k.small_mean) = refs[:6]
    states_in, (k.small, k.small_mom, k.small_avg, k.layer_out, k.in_grad) = refs[6:22], refs[22:27]
    states_out, smalls_out = refs[27:43], refs[43:46]
    (k.fac_ai, k.fac_ao, k.fac_fi, k.fac_fo) = refs[46:50]
    (k.sums, k.weight, k.moment, k.error, k.average, k.approx, k.via_low, k.via_full, k.in_sem, k.out_sem,
     k.pass_sem) = refs[50:]
    passing = [
        (pltpu.make_async_copy(src, via, k.pass_sem.at[n]), pltpu.make_async_copy(via, dst, k.pass_sem.at[3 + n]))
        for n, (src, via, dst) in enumerate(
            ((k.layer_in, k.via_low, k.layer_out), (k.grad_in, k.via_full, k.in_grad))
        )
    ]
    buffers = (k.weight, k.moment, k.error, k.average)
    sums = pltpu.make_async_copy(k.total, k.sums, k.pass_sem.at[2])
    sums.start()
    loads, stores = [
        [
            state_copies(states[4 * n : 4 * n + 4], buffer, sem, 7 * n, outward)
            for n, buffer in enumerate(buffers)
        ]
        for states, sem, outward in ((states_in, k.in_sem, False), (states_out, k.out_sem, True))
    ]
    order = [(0, range(0, 6)), (1, range(6, 8))] + [(2 + c, [8 + c]) for c in range(4)] + [(6, range(12, 16))]
    for n, _ in order:
        for state in loads:
            state[n].start()
    for copy, _ in passing:
        copy.start()
    right = k.right[...]
    k.fac_ai[...] = right[: 6 * RANK].reshape(6, RANK, -1)
    k.fac_ao[...] = right[6 * RANK : 8 * RANK].reshape(2, RANK, -1)
    width = right.shape[1]
    for c in range(4):
        k.fac_fi[0, :, pl.ds(c * width, width)] = right[(8 + c) * RANK : (9 + c) * RANK]
    k.fac_fo[0] = right[12 * RANK :]

    def step(weight, moment, average, update, rate):
        moment_new = MOMENTUM * moment + update
        weight_new = weight - rate * moment_new
        return weight_new, moment_new, average + AVERAGE * (weight_new - average)

    smalls_out[0][...], smalls_out[1][...], smalls_out[2][...] = step(
        k.small[...], k.small_mom[...], k.small_avg[...],
        k.small_mean[pl.ds(0, k.small.shape[0]), :], VECTOR_RATE,
    )
    for piece in range(16):
        slot, factor = (piece, piece) if piece < 8 else (8, piece) if piece < 12 else (piece - 3, 12)
        k.approx[piece] = dot_tn(
            k.own[pl.ds(slot * RANK, RANK), :], right[factor * RANK : (factor + 1) * RANK],
            FULL_PRECISION,
        )
    sums.wait()
    for n, pieces in order:
        for state in loads:
            state[n].wait()
        for piece in pieces:
            approx = k.approx[piece]
            k.error[piece] = k.sums[piece] + k.error[piece] - approx
            k.weight[piece], k.moment[piece], k.average[piece] = step(
                k.weight[piece], k.moment[piece], k.average[piece], approx, LEARN_RATE
            )
        for state in stores:
            state[n].start()
    for incoming, outgoing in passing:
        incoming.wait()
        outgoing.start()
    for state in stores:
        for copy in state:
            copy.wait()
    for _, copy in passing:
        copy.wait()


def local_kernel(*refs):
    b = types.SimpleNamespace()
    (b.sid, b.rank, b.ham, b.dec, b.tgt, b.enc_in, b.og_in) = refs[:7]
    refs = refs[7:]
    b.weights, b.small, layer_out, in_grad_out, b.grads, b.small_grad = (
        refs[:6], refs[6], refs[7], refs[8], refs[9:15], refs[15],
    )
    for key, ref in zip(SCRATCH[:-1], refs[16:]):
        setattr(b, key, ref)
    sem = refs[-1]
    pairs = ((b.dec, b.x), (b.tgt, b.da), (b.enc_in, b.enc), (b.og_in, b.og))
    loads = [pltpu.make_async_copy(src, dst, sem.at[n]) for n, (src, dst) in enumerate(pairs)]
    outs = [pltpu.make_async_copy(b.og, layer_out, sem.at[4]), pltpu.make_async_copy(b.in_grad, in_grad_out, sem.at[5])]
    for copy in loads:
        copy.start()

    def hook(name):
        if name == "inputs":
            for copy in loads:
                copy.wait()
        if name in ("layer_out", "in_grad"):
            outs[name == "in_grad"].start()

    layer_math(b, hook)
    for copy in outs:
        copy.wait()


SCRATCH = list(math_scratch(1024, 512, 2048, 16))
VM = pl.BlockSpec(memory_space=pltpu.VMEM)
HBM = pl.BlockSpec(memory_space=pl.ANY)
SM = pl.BlockSpec(memory_space=pltpu.SMEM)


def padded(small):
    return jnp.pad(small, ((0, 16 - small.shape[0]), (0, 0)))


def run_local(sid, rank, ham, dec, tgt, enc, og, weights, small):
    (length, width), hidden = dec.shape, weights[W1].shape[-1]
    sds = jax.ShapeDtypeStruct
    scratch = math_scratch(length, width, hidden, 16)
    scratch.pop("small_grad")
    grads = [sds(w.shape[:2] + (w.shape[2] * w.shape[3], w.shape[4]), BF) for w in weights]
    return pl.pallas_call(
        local_kernel,
        out_shape=[sds(dec.shape, BF), sds(dec.shape, F32)] + grads + [sds((16, width), F32)],
        in_specs=[VM, VM, SM] + [HBM] * 4 + [VM] * 7,
        out_specs=[HBM, HBM] + [VM] * 7,
        scratch_shapes=list(scratch.values()) + [pltpu.SemaphoreType.DMA((6,))],
        compiler_params=pltpu.CompilerParams(vmem_limit_bytes=VMEM_BYTES),
        name="layer",
    )(sid, rank, ham, dec, tgt, enc, og, *weights, padded(small))


def run_step(chips, acts, weights_in, small_in, errors, factors):
    length, width = acts[3].shape
    hidden = weights_in[2].shape[2]
    sds = jax.ShapeDtypeStruct
    dma = pltpu.SemaphoreType.DMA
    columns = [3 * width, width, 3 * width, width, hidden, width]
    rows = [weights_in[0].shape[1]] * 5 + [weights_in[3].shape[1]]
    slots = 13
    weights = [pltpu.VMEM((chips, 2, 4, r // 4, c), BF) for r, c in zip(rows, columns)]
    grads = [pltpu.VMEM((chips, 2, r, c), BF) for r, c in zip(rows, columns)]
    pair_in = [pltpu.VMEM((chips, r, c), BF) for r, c in zip(rows, columns)]
    land = [pltpu.VMEM((chips - 1, r, c), BF) for r, c in zip(rows, columns)]
    sums = pltpu.VMEM((128, width), F32)
    return pl.pallas_call(
        lambda *refs: step_kernel(chips, *refs),
        out_shape=(
            sds((length, width), BF), sds((length, width), F32), sds((length, width), F32),
            sds((slots * RANK, 64), F32), sds((slots * RANK, width), F32), sds((16, 64), F32),
        ),
        in_specs=[VM, VM, SM] + [HBM] * 8 + [VM] + [HBM] * 4 + [VM] * 4,
        out_specs=(HBM, HBM, HBM, VM, VM, VM),
        scratch_shapes=list(math_scratch(length, width, hidden, 16).values())
        + weights + grads + pair_in + land
        + [
            pltpu.VMEM((16, width), F32), pltpu.VMEM((16, 128), BF), pltpu.VMEM((chips, 16, 128), BF),
            pltpu.VMEM((slots, 4 * RANK, width), BF), pltpu.VMEM((slots * RANK, 64), F32),
            sums, sums, sums, sums,
            pltpu.VMEM((2, 64 + 16 * (chips + 2), width), F32),
            dma((48,)),
            dma((6, chips - 1, 4)), dma((6, chips - 1, 4)), dma((6, chips)), dma((6, chips)),
            dma((6, chips)), dma((6, chips)), dma((2, chips + 7)), dma((2, chips + 7)),
            dma((chips,)), dma((chips,)), dma((3,)),
        ],
        compiler_params=pltpu.CompilerParams(
            vmem_limit_bytes=VMEM_BYTES, collective_id=0, has_side_effects=True
        ),
        name="step",
    )(*acts, *weights_in, small_in, *errors, *factors)


def run_update(layer_out, in_grad, total, own, right, small_mean, states, smalls):
    sds = jax.ShapeDtypeStruct
    like = [sds(s.shape, s.dtype) for group in states for s in group]
    dma = pltpu.SemaphoreType.DMA
    width = right.shape[1]
    state = pltpu.VMEM((16, 64, width), F32)
    faced = [sds(s, F32) for s in ((6, RANK, width), (2, RANK, width), (1, RANK, 4 * width), (1, RANK, width))]
    return pl.pallas_call(
        update_kernel,
        out_shape=[sds(layer_out.shape, layer_out.dtype), sds(in_grad.shape, in_grad.dtype)]
        + like + [sds(s.shape, F32) for s in smalls] + faced,
        in_specs=[HBM] * 3 + [VM] * 3 + [HBM] * 16 + [VM] * 3,
        out_specs=[HBM] * 18 + [VM] * 7,
        scratch_shapes=[state] * 6
        + [pltpu.VMEM(layer_out.shape, BF), pltpu.VMEM(in_grad.shape, F32)]
        + [dma((28,)), dma((28,)), dma((5,))],
        compiler_params=pltpu.CompilerParams(vmem_limit_bytes=VMEM_BYTES),
        name="update",
    )(layer_out, in_grad, total, own, right, small_mean, *[s for group in states for s in group], *smalls)


def fused_body(
    chips, decoder_input, target_embed, encoder_states, sentence_ids, position_ranks, hamming_counts,
    output_grad, attn_in, attn_out, ffn_in, ffn_out, small_params, attn_in_mom, attn_out_mom, ffn_in_mom,
    ffn_out_mom, small_mom, attn_in_err, attn_out_err, ffn_in_err, ffn_out_err, attn_in_fac, attn_out_fac,
    ffn_in_fac, ffn_out_fac, attn_in_avg, attn_out_avg, ffn_in_avg, ffn_out_avg, small_avg,
):
    masters = [attn_in, attn_out, ffn_in, ffn_out]
    errors = [attn_in_err[0], attn_out_err[0], ffn_in_err[0], ffn_out_err[0]]
    factors = [jnp.swapaxes(f, 1, 2) for f in (attn_in_fac, attn_out_fac, ffn_in_fac, ffn_out_fac)]
    acts = [
        sentence_ids, position_ranks, hamming_counts,
        decoder_input[0], target_embed[0], encoder_states[0], output_grad[0],
    ]
    layer_out, in_grad, total, own, right, small_mean = run_step(
        chips, acts, masters, small_params, errors, factors
    )
    width = right.shape[1]

    def pieces(group):
        return [group[0], group[1], group[2], group[3].reshape(4, 64, width)]

    states = [
        pieces(masters),
        pieces([attn_in_mom, attn_out_mom, ffn_in_mom, ffn_out_mom]),
        pieces(errors),
        pieces([attn_in_avg, attn_out_avg, ffn_in_avg, ffn_out_avg]),
    ]
    found = run_update(
        layer_out, in_grad, total.reshape(16, 64, width), own, right, small_mean, states,
        [small_params, small_mom, small_avg],
    )
    layer_out, in_grad, found = found[0], found[1], found[2:]
    new = [list(found[4 * n : 4 * n + 4]) for n in range(4)]
    for group in new:
        group[3] = group[3].reshape(ffn_out.shape)
    weights, moments, errs, averages = new
    small_new, small_mom_new, small_avg_new = found[16:19]
    fac = [jnp.swapaxes(f, 1, 2) for f in found[19:]]
    return (
        layer_out[None], in_grad[None], *weights, small_new, *moments, small_mom_new,
        *[e[None] for e in errs], *fac, *averages, small_avg_new,
    )


def body(
    decoder_input,
    target_embed,
    encoder_states,
    sentence_ids,
    position_ranks,
    hamming_counts,
    output_grad,
    attn_in,
    attn_out,
    ffn_in,
    ffn_out,
    small_params,
    attn_in_mom,
    attn_out_mom,
    ffn_in_mom,
    ffn_out_mom,
    small_mom,
    attn_in_err,
    attn_out_err,
    ffn_in_err,
    ffn_out_err,
    attn_in_fac,
    attn_out_fac,
    ffn_in_fac,
    ffn_out_fac,
    attn_in_avg,
    attn_out_avg,
    ffn_in_avg,
    ffn_out_avg,
    small_avg,
):
    small_full = lax.all_gather(
        small_params.astype(BF), "wide", axis=1, tiled=True
    ).astype(F32)

    def columns(stack):
        return jnp.swapaxes(stack, 0, 1).reshape(stack.shape[1], -1)

    def gather(rows):
        return lax.all_gather(rows.astype(BF), "wide", axis=0, tiled=True)

    whole = [
        gather(columns(attn_in[:3])), gather(attn_out[0]),
        gather(columns(attn_in[3:])), gather(attn_out[1]),
        gather(ffn_in[0]), gather(ffn_out[0]),
    ]
    length = decoder_input.shape[1]
    layer_out, input_grad, *grads, small_grad = run_local(
        sentence_ids, position_ranks, hamming_counts, decoder_input[0], target_embed[0],
        encoder_states[0], output_grad[0],
        [w.reshape(4, 2, 4, -1, w.shape[1]) for w in whole], small_full,
    )
    ga1, go1, ga2, go2, g1, g2 = [g.reshape(-1, g.shape[-1]) for g in grads]
    small_grad = small_grad[: small_full.shape[0]]

    def scatter(rows):
        return lax.psum_scatter(rows, "wide", scatter_dimension=0, tiled=True).astype(F32)

    def stack_of(rows):
        return jnp.swapaxes(rows.reshape(rows.shape[0], -1, g1.shape[0]), 0, 1)

    second, first = scatter(g2), scatter(g1)
    out_two, in_two, out_one, in_one = scatter(go2), scatter(ga2), scatter(go1), scatter(ga1)
    shards = (
        jnp.concatenate([stack_of(in_one), stack_of(in_two)], axis=0),
        jnp.stack([out_one, out_two]),
        first[None],
        second[None],
        lax.psum_scatter(small_grad, "wide", scatter_dimension=1, tiled=True),
    )
    scaling = (length * lax.axis_size("wide")) ** (-0.5)
    replicas = lax.axis_size("rep")
    fulls, lefts = ([], [])
    for gradient, error, factor_in in zip(
        shards[:4],
        (attn_in_err, attn_out_err, ffn_in_err, ffn_out_err),
        (attn_in_fac, attn_out_fac, ffn_in_fac, ffn_out_fac),
    ):
        full_grad = gradient * scaling + error[0]
        fulls.append(full_grad)
        lefts.append(jnp.einsum("knm,kmq->knq", full_grad, factor_in, precision=FULL_PRECISION))
    summed = lax.psum((lefts[0], lefts[1], lefts[2], lefts[3], shards[4] * scaling), "rep")
    left_mean = [piece / replicas for piece in summed[:4]]
    local_grams = [
        jnp.einsum("knq,kns->kqs", piece, piece, precision=FULL_PRECISION) for piece in left_mean
    ]
    grams = lax.psum((local_grams[0], local_grams[1], local_grams[2], local_grams[3]), "wide")
    orthos, rights = ([], [])
    for full_grad, piece, gram in zip(fulls, left_mean, grams):
        cholesky_factor = jnp.linalg.cholesky(gram)
        orthonormal = jnp.swapaxes(
            jax.scipy.linalg.solve_triangular(
                cholesky_factor, jnp.swapaxes(piece, 1, 2), lower=True
            ),
            1,
            2,
        )
        orthos.append(orthonormal)
        rights.append(jnp.einsum("knm,knq->kmq", full_grad, orthonormal, precision=FULL_PRECISION))
    right_sums = lax.psum((rights[0], rights[1], rights[2], rights[3]), ("rep", "wide"))
    reduced, new_errors, new_factors = ([], [], [])
    for full_grad, orthonormal, right_sum in zip(fulls, orthos, right_sums):
        right_mean = right_sum / replicas
        approx = jnp.einsum("knq,kmq->knm", orthonormal, right_mean, precision=FULL_PRECISION)
        reduced.append(approx)
        new_errors.append((full_grad - approx)[None])
        new_factors.append(right_mean)
    reduced.append(summed[4] / replicas)
    masters = (attn_in, attn_out, ffn_in, ffn_out, small_params)
    momenta = (attn_in_mom, attn_out_mom, ffn_in_mom, ffn_out_mom, small_mom)
    averages = (attn_in_avg, attn_out_avg, ffn_in_avg, ffn_out_avg, small_avg)
    rates = (LEARN_RATE, LEARN_RATE, LEARN_RATE, LEARN_RATE, VECTOR_RATE)
    new_weights, new_momenta, new_averages = ([], [], [])
    for master, moment, average, update, rate in zip(masters, momenta, averages, reduced, rates):
        moment_new = MOMENTUM * moment + update
        weight_new = master - rate * moment_new
        new_weights.append(weight_new)
        new_momenta.append(moment_new)
        new_averages.append(average + AVERAGE * (weight_new - average))
    return (
        layer_out[None],
        input_grad[None],
        new_weights[0],
        new_weights[1],
        new_weights[2],
        new_weights[3],
        new_weights[4],
        new_momenta[0],
        new_momenta[1],
        new_momenta[2],
        new_momenta[3],
        new_momenta[4],
        new_errors[0],
        new_errors[1],
        new_errors[2],
        new_errors[3],
        new_factors[0],
        new_factors[1],
        new_factors[2],
        new_factors[3],
        new_averages[0],
        new_averages[1],
        new_averages[2],
        new_averages[3],
        new_averages[4],
    )


def solution(mesh):
    placed = (
        P(("rep", "wide"), None, None),
        P(("rep", "wide"), None, None),
        P(("rep", "wide"), None, None),
        P(("rep", "wide"), None),
        P(("rep", "wide"), None),
        P(("rep", "wide"), None),
        P(("rep", "wide"), None, None),
        P(None, "wide", None),
        P(None, "wide", None),
        P(None, "wide", None),
        P(None, "wide", None),
        P(None, "wide"),
        P(None, "wide", None),
        P(None, "wide", None),
        P(None, "wide", None),
        P(None, "wide", None),
        P(None, "wide"),
        P("rep", None, "wide", None),
        P("rep", None, "wide", None),
        P("rep", None, "wide", None),
        P("rep", None, "wide", None),
        P(),
        P(),
        P(),
        P(),
        P(None, "wide", None),
        P(None, "wide", None),
        P(None, "wide", None),
        P(None, "wide", None),
        P(None, "wide"),
    )
    wide = mesh.shape["wide"]
    fused = mesh.shape["rep"] == 4 and wide == 8
    return jax.shard_map(
        functools.partial(fused_body, wide // 2) if fused else body,
        mesh=mesh,
        in_specs=placed,
        out_specs=(
            P(("rep", "wide"), None, None),
            P(("rep", "wide"), None, None),
            P(None, "wide", None),
            P(None, "wide", None),
            P(None, "wide", None),
            P(None, "wide", None),
            P(None, "wide"),
            P(None, "wide", None),
            P(None, "wide", None),
            P(None, "wide", None),
            P(None, "wide", None),
            P(None, "wide"),
            P("rep", None, "wide", None),
            P("rep", None, "wide", None),
            P("rep", None, "wide", None),
            P("rep", None, "wide", None),
            P(),
            P(),
            P(),
            P(),
            P(None, "wide", None),
            P(None, "wide", None),
            P(None, "wide", None),
            P(None, "wide", None),
            P(None, "wide"),
        ),
        check_vma=False,
    )
```
